256 devices in a mesh: rep: 8 (over y_lo, x), fsdp: 32 (over z, y_hi, core).
Axes of the slice: x: 4, y: 4 (y_hi: 2, y_lo: 2; y = y_hi * 2 + y_lo), z: 8, core: 2. Of those that a mesh axis runs over, the one named last changes fastest.
Arguments:
- hidden: bfloat16 [8, 12288, 8192], P('rep', 'fsdp'), may hold values from -6 to 6
- token_ids: int32 [8, 12288], P('rep', 'fsdp'), may hold values from 0 to 128255, as said below
- key_grad: bfloat16 [8, 12288, 512], P('rep', 'fsdp')
- weights: float32 [8, 8192, 512], P('rep', 'fsdp'), may hold values from -6 to 6
- first_moment: float32 [8, 8192, 512], P('rep', 'fsdp'), may hold values from -6 to 6
- second_moment: float32 [8, 8192, 512], P('rep', 'fsdp'), may hold values from 0.25 to 4
- anchor: float32 [8192, 512], P('fsdp'), may hold values from -6 to 6
- momentum: float32 [8192, 512], P('fsdp'), may hold values from -3 to 3
- fragment: int32 [1], replicated, may hold values from 0 to 1
- step_count: int32 [1], replicated, may hold values from 2 to 23
Outputs:
- keys: bfloat16 [8, 12288, 512], P('rep', 'fsdp')
- new_weights: float32 [8, 8192, 512], P('rep', 'fsdp')
- new_first: float32 [8, 8192, 512], P('rep', 'fsdp')
- new_second: float32 [8, 8192, 512], P('rep', 'fsdp')
- new_anchor: float32 [8192, 512], P('fsdp')
- new_momentum: float32 [8192, 512], P('fsdp')
The draws below stay inside these ranges and needn't reach their ends.
Inputs may be any that keep to these rules, and one draw needn't show every extreme that they name: `token_ids`: 0 marks an empty slot; any other value is a vocabulary id below 128256.
All inputs are finite; a program needn't handle non-finite values.
Results may differ from the reference program's by a relative error of at most 0.0049.
Values may be sent and summed in bfloat16 or wider, within the bound.
A program may use at most 128 MiB of HBM per device.

```python
import math
import jax
import jax.numpy as jnp
from jax import lax

D = 8192
KVW = 512
VOCAB = 128256
FRAGS = 2
TOK_DEV = 384
FW = 256
GROUPS = 8
TOKENS_G = 12288


def draw_token_ids(key, part):
    key = jax.random.fold_in(key, 11)
    coin_key, value_key = jax.random.split(key)
    device_rows = jnp.arange(TOKENS_G, dtype=jnp.int32) // TOK_DEV
    span_devices = max(TOKENS_G // TOK_DEV - 1, 1)
    thresholds = 250 + 500 * device_rows // span_devices
    coin_flips = jax.random.randint(coin_key, (GROUPS, TOKENS_G), 0, 1000)
    vocab_ids = jax.random.randint(value_key, (GROUPS, TOKENS_G), 1, VOCAB)
    drawn = jnp.where(coin_flips < thresholds[None, :], vocab_ids, 0).astype(jnp.int32)
    return drawn.at[:, TOKENS_G - 1].set(VOCAB - 1).astype(jnp.int32)


def draw_key_grad(key, part):
    key = jax.random.fold_in(key, 23)
    grad_scale = math.sqrt(D * TOKENS_G / 2.0)
    values = jax.random.normal(key, (GROUPS, TOKENS_G, KVW), jnp.float32)
    return (values * grad_scale).astype(jnp.bfloat16)


def block_scale(own_key, shape, shards, low, largest):
    gain = 1.0
    for dim, blocks in shards:
        draws = jax.random.uniform(jax.random.fold_in(jax.random.fold_in(own_key, 6), dim), (blocks,), jnp.float32, low / len(shards), largest / len(shards))
        gain = gain * jnp.repeat(jnp.exp(draws), shape[dim] // blocks).reshape((-1,) + (1,) * (len(shape) - 1 - dim))
    return gain


def bell_draw(key, shape, scale, most, shards=(), kind=jnp.bfloat16):
    factor_of = block_scale(key, shape, shards, -0.22, 0.18) if shards else 1.0
    values = jax.random.normal(key, shape, jnp.float32) * scale * factor_of
    return jnp.minimum(jnp.maximum(values, -most), most).astype(kind)


def setup_inputs(seed: int = 0) -> dict:
    seeds = jax.random.split(jax.random.key(seed), 11)
    return {
        "hidden": bell_draw(seeds[0], (GROUPS, TOKENS_G, D), 1.0, 6.0, ((0, 8), (1, 32))),
        "token_ids": draw_token_ids(jax.random.fold_in(seeds[10], 71), 0),
        "key_grad": draw_key_grad(jax.random.fold_in(seeds[10], 71), 0),
        "weights": bell_draw(seeds[3], (GROUPS, D, KVW), 1.0, 6.0, ((0, 8), (1, 32)), jnp.float32),
        "first_moment": bell_draw(seeds[4], (GROUPS, D, KVW), 1.0, 6.0, ((0, 8), (1, 32)), jnp.float32),
        "second_moment": jnp.clip(jnp.exp(math.log(4.0) - 2.7725887 * jax.random.uniform(seeds[5], (GROUPS, D, KVW), jnp.float32) ** block_scale(seeds[5], (GROUPS, D, KVW), ((0, 8), (1, 32)), -0.2, 0.2)), 0.25, 4.0),
        "anchor": bell_draw(seeds[6], (D, KVW), 1.0, 6.0, ((0, 32),), jnp.float32),
        "momentum": bell_draw(seeds[7], (D, KVW), 0.5, 3.0, ((0, 32),), jnp.float32),
        "fragment": jax.random.randint(seeds[8], (1,), 0, FRAGS).astype(jnp.int32),
        "step_count": jax.random.randint(seeds[9], (1,), 2, 24).astype(jnp.int32),
    }


BETA_ONE = 0.9
BETA_TWO = 0.95
EPSILON = 1e-08
INNER_LR = 0.1
WEIGHT_DECAY = 0.1
OUTER_LR = 0.7
OUTER_MOMENTUM = 0.9
MIX_LOCAL = 0.5

def reference(hidden, token_ids, key_grad, weights, first_moment, second_moment, anchor, momentum, fragment, step_count):
    inverse_root = 1.0 / math.sqrt(D)
    live_mask = token_ids != 0
    live_counts = lax.optimization_barrier(jnp.sum(live_mask.astype(jnp.float32), axis=1))

    def one_group(operands):
        tokens, group_weights, group_grads, group_live, group_count = operands
        key_sums = jnp.dot(tokens, group_weights.astype(jnp.bfloat16), preferred_element_type=jnp.float32)
        group_keys = (key_sums * inverse_root).astype(jnp.bfloat16)
        masked = group_grads * group_live[:, None].astype(jnp.bfloat16)
        grad_sum = jnp.dot(tokens.T, masked, preferred_element_type=jnp.float32)
        return (group_keys, grad_sum * inverse_root / group_count)
    new_keys, gradient = lax.map(one_group, (hidden, weights, key_grad, live_mask, live_counts))
    step_float = step_count[0].astype(jnp.float32)
    new_first = BETA_ONE * first_moment + (1.0 - BETA_ONE) * gradient
    new_second = BETA_TWO * second_moment + (1.0 - BETA_TWO) * gradient * gradient
    ratio_term = new_first / (1.0 - BETA_ONE ** step_float) / (jnp.sqrt(new_second / (1.0 - BETA_TWO ** step_float)) + EPSILON)
    stepped = weights - INNER_LR * (ratio_term + WEIGHT_DECAY * weights)
    first_col = (fragment[0] * FW).astype(jnp.int32)
    differences = lax.dynamic_slice_in_dim(anchor[None] - weights, first_col, FW, 2)
    delta = lax.optimization_barrier(jnp.sum(differences, axis=0)) / GROUPS
    momentum_cols = lax.dynamic_slice_in_dim(momentum, first_col, FW, 1)
    anchor_cols = lax.dynamic_slice_in_dim(anchor, first_col, FW, 1)
    moved_momentum = OUTER_MOMENTUM * momentum_cols + delta
    moved_anchor = anchor_cols - OUTER_LR * (delta + OUTER_MOMENTUM * moved_momentum)
    stepped_cols = lax.dynamic_slice_in_dim(stepped, first_col, FW, 2)
    mixed_cols = MIX_LOCAL * stepped_cols + (1.0 - MIX_LOCAL) * moved_anchor[None]
    new_weights = lax.dynamic_update_slice_in_dim(stepped, mixed_cols, first_col, 2)
    new_anchor = lax.dynamic_update_slice_in_dim(anchor, moved_anchor, first_col, 1)
    new_momentum = lax.dynamic_update_slice_in_dim(momentum, moved_momentum, first_col, 1)
    return (new_keys, new_weights, new_first, new_second, new_anchor, new_momentum)
```

```python
import math

import jax
import jax.numpy as jnp
from jax import lax
from jax.experimental import pallas as pl
from jax.experimental.pallas import tpu as pltpu
from jax.sharding import PartitionSpec as P

MESH = pl.DeviceIdType.MESH
BF16, F32 = jnp.bfloat16, jnp.float32

D = 8192
FRAGS = 2
NZ = 8
BLOCK = 256
ROWS_A = 128
ROWS_B = BLOCK - ROWS_A
STEP = 32

BETA_ONE = 0.9
BETA_TWO = 0.95
EPSILON = 1e-08
INNER_LR = 0.1
WEIGHT_DECAY = 0.1
OUTER_LR = 0.7
OUTER_MOMENTUM = 0.9
MIX_LOCAL = 0.5


def order(d):
    return {4: 0, 3: 1, -3: 2, 2: 3, -2: 4, 1: 5, -1: 6, 0: 7}[d]


def slot(d, p):
    return 2 * order(d) + p


def distance(o):
    far = 4 - (o + 1) // 2
    return jnp.where(o % 2 == 1, far, -far)


def kernel(
    hidden, masked, weights, grad_out, keys_out,
    held, grads_in, parts, wire, acc, other, send_z, recv_z, send_y, recv_y, send_a, recv_a,
    local_sem, send_sem, recv_sem, hid_send, hid_recv,
):
    tok = masked.shape[0]
    width = masked.shape[1]
    half = width // 2
    rep = lax.axis_index("rep")
    me = lax.axis_index("fsdp")
    z, yh, core = me // 4, (me // 2) % 2, me % 2
    mate = (rep, z * 4 + yh * 2 + (1 - core))
    across = (rep, z * 4 + (1 - yh) * 2 + core)
    up = (rep, lax.rem(z + 1, NZ) * 4 + yh * 2 + core)
    down = (rep, lax.rem(z + NZ - 1, NZ) * 4 + yh * 2 + core)
    toward = {1: up, -1: down}
    rows_a, rows_b = pl.ds(0, ROWS_A), pl.ds(ROWS_A, ROWS_B)
    cols = {1: pl.ds(0, half), -1: pl.ds(half, half)}
    copies = {}

    def block_cols(q, c):
        d, p = distance(q // 2), q % 2
        zz = lax.rem(z + d + 2 * NZ, NZ)
        yy = lax.rem(yh + p, 2)
        return pl.ds(pl.multiple_of((zz * 4 + yy * 2 + c) * BLOCK, BLOCK), BLOCK)

    def hidden_local(q):
        return pltpu.make_async_copy(
            hidden.at[:, block_cols(q, core)], held.at[q, pl.ds(0, tok)], local_sem.at[q]
        )

    def hidden_remote(q):
        return pltpu.make_async_remote_copy(
            src_ref=hidden.at[:, block_cols(q, 1 - core)],
            dst_ref=held.at[q, pl.ds(tok, tok)],
            send_sem=hid_send.at[q],
            recv_sem=hid_recv.at[q],
            device_id=mate,
            device_id_type=MESH,
        )

    def send(name, src, dst, target):
        index = len(copies)
        copies[name] = pltpu.make_async_remote_copy(
            src_ref=src,
            dst_ref=dst,
            send_sem=send_sem.at[index],
            recv_sem=recv_sem.at[index],
            device_id=target,
            device_id_type=MESH,
        )
        copies[name].start()

    def arrived(name):
        copies[name].wait_recv()

    def loop_rows(count, body):
        @pl.loop(0, count // STEP)
        def _(i):
            body(pl.multiple_of(i * STEP, STEP))

    @pl.loop(0, 16)
    def _(q):
        hidden_local(q).start()

    barrier = pltpu.get_barrier_semaphore()
    for target in (mate, across, up, down):
        pl.semaphore_signal(barrier, inc=1, device_id=target, device_id_type=MESH)
    own = slot(0, 0)

    def cast(r):
        wire[own, pl.ds(r, STEP)] = weights[pl.ds(r, STEP)].astype(BF16)

    loop_rows(BLOCK, cast)

    def take(r):
        grads_in[pl.ds(r, STEP)] = masked[pl.ds(r, STEP)]

    loop_rows(tok, take)
    pl.semaphore_wait(barrier, 4)

    send("ay0", wire.at[own, rows_a], wire.at[slot(0, 1), rows_a], across)
    for s in (1, -1):
        send(("az", s, 1, 0), wire.at[own], wire.at[slot(-s, 0)], toward[s])
    send("ayB0", wire.at[own, rows_b], wire.at[slot(0, 1), rows_b], across)
    send("mask", grads_in.at[pl.ds(0, tok)], grads_in.at[pl.ds(tok, tok)], mate)

    @pl.loop(0, 16)
    def _(q):
        hidden_remote(q).start()

    def gather_hop(k, p):
        for s in (1, -1):
            src = slot(-s * (k - 1), p)
            dst = slot(4 if k == 4 else -s * k, p)
            rows = pl.ds(0, BLOCK) if p == 0 else rows_a
            if k > 1:
                arrived(("az", s, k - 1, p))
            if k == 4:
                send(("az", s, k, p), wire.at[src, rows, cols[s]], wire.at[dst, rows, cols[s]], toward[s])
            else:
                send(("az", s, k, p), wire.at[src, rows], wire.at[dst, rows], toward[s])
            if p == 0 and k > 1:
                send(("ayB", src), wire.at[src, rows_b], wire.at[src + 1, rows_b], across)

    def gather_step(k):
        gather_hop(k, 0)
        gather_hop(k, 1)

    def gradient(*distances):
        first = order(distances[0])

        @pl.loop(2 * first, 2 * (first + len(distances)))
        def _(q):
            hidden_local(q).wait()
            hidden_remote(q).wait_recv()
            parts[q] = lax.dot_general(
                held[q], grads_in[...], (((0,), (0,)), ((), ())), preferred_element_type=F32
            )

        for d in distances:
            o = order(d)

            def stage(r, o=o):
                send_y[o, pl.ds(r, STEP)] = parts[2 * o + 1, pl.ds(ROWS_A + r, STEP)].astype(BF16)

            loop_rows(ROWS_B, stage)
            send(("ry", d), send_y.at[o], recv_y.at[o], across)

    def reduce_far(p):
        for s in (1, -1):
            def stage(r, s=s):
                here = parts[slot(4, p), pl.ds(r, STEP), cols[s]]
                send_z[0 if s == 1 else 1, 3, pl.ds(p * BLOCK + r, STEP), cols[s]] = here.astype(BF16)

            def stage_b(r, s=s):
                here = parts[slot(4, p), pl.ds(ROWS_A + r, STEP), cols[s]]
                here = here + recv_y[order(4), pl.ds(r, STEP), cols[s]].astype(F32)
                send_z[0 if s == 1 else 1, 3, pl.ds(ROWS_A + r, STEP), cols[s]] = here.astype(BF16)

            loop_rows(ROWS_A, stage)
            if p == 0:
                if s == 1:
                    arrived(("ry", 4))
                loop_rows(ROWS_B, stage_b)
            rows = pl.ds(0, BLOCK) if p == 0 else pl.ds(BLOCK, ROWS_A)
            w = 0 if s == 1 else 1
            send(("rz", s, 4, p), send_z.at[w, 3, rows, cols[s]], recv_z.at[w, 3, rows, cols[s]], toward[s])

    def reduce_hop(d, p):
        for s in (1, -1):
            w = 0 if s == 1 else 1
            arrived(("rz", s, d + 1, p))
            if p == 0:
                arrived(("ry", s * d))

            def put(r, base, with_y, s=s, w=w):
                here = parts[slot(s * d, p), pl.ds(base + r, STEP)]
                at = pl.ds(p * BLOCK + base + r, STEP)
                if with_y:
                    here = here + recv_y[order(s * d), pl.ds(r, STEP)].astype(F32)
                if d == 3:
                    lo = 0 if s == 1 else half
                    there = recv_z[w, d, at, cols[s]].astype(F32)
                    summed = here[:, lo:lo + half] + there
                    send_z[w, d - 1, at, cols[s]] = summed.astype(BF16)
                    send_z[w, d - 1, at, cols[-s]] = here[:, half - lo:2 * half - lo].astype(BF16)
                else:
                    there = recv_z[w, d, at].astype(F32)
                    send_z[w, d - 1, at] = (here + there).astype(BF16)

            loop_rows(ROWS_A, lambda r: put(r, 0, False))
            if p == 0:
                loop_rows(ROWS_B, lambda r: put(r, ROWS_A, True))
            rows = pl.ds(0, BLOCK) if p == 0 else pl.ds(BLOCK, ROWS_A)
            send(("rz", s, d, p), send_z.at[w, d - 1, rows], recv_z.at[w, d - 1, rows], toward[s])

    def keys(*distances):
        for d in distances:
            q = slot(d, 0)
            if d == 0:
                arrived("ayB0")
            elif d == 4:
                arrived(("ayB", 4, 1))
                arrived(("ayB", 4, -1))
            else:
                arrived(("ayB", q))
            acc[...] += jnp.dot(held[q], wire[q], preferred_element_type=F32) + jnp.dot(
                held[q + 1], wire[q + 1], preferred_element_type=F32
            )

    arrived("mask")
    gradient(4)
    reduce_far(1)
    arrived("ay0")
    gather_hop(1, 1)
    gradient(3, -3)
    reduce_far(0)
    gather_step(2)
    gradient(2, -2)
    reduce_hop(3, 1)
    reduce_hop(3, 0)
    gather_step(3)
    gradient(1, -1, 0)
    acc[...] = jnp.zeros_like(acc)
    reduce_hop(2, 1)
    reduce_hop(2, 0)
    gather_step(4)
    keys(0)
    reduce_hop(1, 1)
    reduce_hop(1, 0)
    for s in (1, -1):
        arrived(("az", s, 4, 0))
        src = slot(4, 0)
        send(("ayB", 4, s), wire.at[src, rows_b, cols[s]], wire.at[src + 1, rows_b, cols[s]], across)
    keys(1, -1, 2, -2, 3, -3)

    for s in (1, -1):
        arrived(("rz", s, 1, 1))

    def close_a(r):
        at = pl.ds(BLOCK + r, STEP)
        total = parts[slot(0, 1), pl.ds(r, STEP)] + recv_z[0, 0, at].astype(F32) + recv_z[1, 0, at].astype(F32)
        send_a[pl.ds(r, STEP)] = total.astype(BF16)

    loop_rows(ROWS_A, close_a)
    send("rya", send_a, recv_a, across)
    for s in (1, -1):
        arrived(("az", s, 4, 1))
    keys(4)
    send("keys", acc.at[pl.ds(tok, tok)], other, mate)
    for s in (1, -1):
        arrived(("rz", s, 1, 0))
    arrived(("ry", 0))

    def close_b(r):
        at = pl.ds(ROWS_A + r, STEP)
        total = parts[slot(0, 0), at] + recv_y[order(0), pl.ds(r, STEP)].astype(F32)
        grad_out[at] = total + recv_z[0, 0, at].astype(F32) + recv_z[1, 0, at].astype(F32)

    loop_rows(ROWS_B, close_b)
    arrived("rya")

    def close_all(r):
        at = pl.ds(r, STEP)
        total = parts[slot(0, 0), at] + recv_a[at].astype(F32)
        grad_out[at] = total + recv_z[0, 0, at].astype(F32) + recv_z[1, 0, at].astype(F32)

    loop_rows(ROWS_A, close_all)
    arrived("keys")

    def close_keys(r):
        at = pl.ds(r, STEP)
        keys_out[at] = ((acc[at] + other[at]) * (1.0 / math.sqrt(D))).astype(BF16)

    loop_rows(tok, close_keys)
    for copy in copies.values():
        copy.wait_send()

    @pl.loop(0, 16)
    def _(q):
        hidden_remote(q).wait_send()


def exchange(hidden, masked, weights):
    tok, width = masked.shape
    vmem = pl.BlockSpec(memory_space=pltpu.VMEM)
    count = 80
    return pl.pallas_call(
        kernel,
        out_shape=(
            jax.ShapeDtypeStruct((BLOCK, width), F32),
            jax.ShapeDtypeStruct((tok, width), BF16),
        ),
        in_specs=[pl.BlockSpec(memory_space=pl.ANY), vmem, vmem],
        out_specs=(vmem, vmem),
        scratch_shapes=[
            pltpu.VMEM((16, 2 * tok, BLOCK), BF16),
            pltpu.VMEM((2 * tok, width), BF16),
            pltpu.VMEM((16, BLOCK, width), F32),
            pltpu.VMEM((16, BLOCK, width), BF16),
            pltpu.VMEM((2 * tok, width), F32),
            pltpu.VMEM((tok, width), F32),
            pltpu.VMEM((2, 4, BLOCK + ROWS_A, width), BF16),
            pltpu.VMEM((2, 4, BLOCK + ROWS_A, width), BF16),
            pltpu.VMEM((8, ROWS_B, width), BF16),
            pltpu.VMEM((8, ROWS_B, width), BF16),
            pltpu.VMEM((ROWS_A, width), BF16),
            pltpu.VMEM((ROWS_A, width), BF16),
            pltpu.SemaphoreType.DMA((16,)),
            pltpu.SemaphoreType.DMA((count,)),
            pltpu.SemaphoreType.DMA((count,)),
            pltpu.SemaphoreType.DMA((16,)),
            pltpu.SemaphoreType.DMA((16,)),
        ],
        compiler_params=pltpu.CompilerParams(
            collective_id=0, has_side_effects=True, vmem_limit_bytes=56 * 2**20
        ),
        cost_estimate=pl.CostEstimate(flops=13 * 10**9, bytes_accessed=16 * 2**20, transcendentals=0),
    )(hidden, masked, weights)


def on_device(
    hidden,
    token_ids,
    key_grad,
    weights,
    first_moment,
    second_moment,
    anchor,
    momentum,
    fragment,
    step_count,
):
    inverse_root = 1.0 / math.sqrt(D)
    own_weights = weights[0]
    key_width = own_weights.shape[1]
    frag_width = key_width // FRAGS
    first_col = fragment[0] * frag_width
    live_mask = token_ids[0] != 0
    local_count = jnp.sum(live_mask.astype(F32))
    group_count = lax.psum(local_count, "fsdp")
    own_delta = lax.dynamic_slice_in_dim(anchor - own_weights, first_col, frag_width, 1)
    delta = lax.psum(own_delta, "rep") / lax.axis_size("rep")
    masked = key_grad[0] * live_mask[:, None].astype(BF16)
    grad_sum, new_keys = exchange(hidden[0], masked, own_weights)
    gradient = grad_sum * inverse_root / group_count
    step_float = step_count[0].astype(F32)
    new_first = BETA_ONE * first_moment[0] + (1.0 - BETA_ONE) * gradient
    new_second = BETA_TWO * second_moment[0] + (1.0 - BETA_TWO) * gradient * gradient
    ratio_term = (
        new_first
        / (1.0 - BETA_ONE**step_float)
        / (jnp.sqrt(new_second / (1.0 - BETA_TWO**step_float)) + EPSILON)
    )
    stepped = own_weights - INNER_LR * (ratio_term + WEIGHT_DECAY * own_weights)
    momentum_cols = lax.dynamic_slice_in_dim(momentum, first_col, frag_width, 1)
    anchor_cols = lax.dynamic_slice_in_dim(anchor, first_col, frag_width, 1)
    moved_momentum = OUTER_MOMENTUM * momentum_cols + delta
    moved_anchor = anchor_cols - OUTER_LR * (delta + OUTER_MOMENTUM * moved_momentum)
    stepped_cols = lax.dynamic_slice_in_dim(stepped, first_col, frag_width, 1)
    mixed_cols = MIX_LOCAL * stepped_cols + (1.0 - MIX_LOCAL) * moved_anchor
    new_weights = lax.dynamic_update_slice_in_dim(stepped, mixed_cols, first_col, 1)
    new_anchor = lax.dynamic_update_slice_in_dim(anchor, moved_anchor, first_col, 1)
    new_momentum = lax.dynamic_update_slice_in_dim(momentum, moved_momentum, first_col, 1)
    return (
        new_keys[None],
        new_weights[None],
        new_first[None],
        new_second[None],
        new_anchor,
        new_momentum,
    )


def solution(mesh):
    return jax.shard_map(
        on_device,
        mesh=mesh,
        in_specs=(
            P("rep", "fsdp", None),
            P("rep", "fsdp"),
            P("rep", "fsdp", None),
            P("rep", "fsdp", None),
            P("rep", "fsdp", None),
            P("rep", "fsdp", None),
            P("fsdp", None),
            P("fsdp", None),
            P(),
            P(),
        ),
        out_specs=(
            P("rep", "fsdp", None),
            P("rep", "fsdp", None),
            P("rep", "fsdp", None),
            P("rep", "fsdp", None),
            P("fsdp", None),
            P("fsdp", None),
        ),
        check_vma=False,
    )
```

```python
import math

import jax
import jax.numpy as jnp
from jax import lax
from jax.experimental import pallas as pl
from jax.experimental.pallas import tpu as pltpu
from jax.sharding import PartitionSpec as P

MESH = pl.DeviceIdType.MESH
BF16, F32 = jnp.bfloat16, jnp.float32

D = 8192
FRAGS = 2
NZ = 8
NX = 4
BLOCK = 256
ROWS_A = 112
ROWS_B = BLOCK - ROWS_A
STEP = 16

BETA_ONE = 0.9
BETA_TWO = 0.95
EPSILON = 1e-08
INNER_LR = 0.1
WEIGHT_DECAY = 0.1
OUTER_LR = 0.7
OUTER_MOMENTUM = 0.9
MIX_LOCAL = 0.5


def order(d):
    return {4: 0, 3: 1, -3: 2, 2: 3, -2: 4, 1: 5, -1: 6, 0: 7}[d]


def slot(d, p):
    return 2 * order(d) + p


def distance(o):
    far = 4 - (o + 1) // 2
    return jnp.where(o % 2 == 1, far, -far)


def kernel(
    hidden, tokens, key_grad, weights, anchor, fragment, grad_out, keys_out, delta_out,
    held, grads_in, parts, wire, acc, other, send_z, recv_z, send_y, recv_y, send_a, recv_a,
    raw_grad, raw_weights, raw_anchor, raw_tokens, differ, from_x, piece, from_y, delta, counts, count_mate, count_pair, count_across,
    local_sem, raw_sem, send_sem, recv_sem, hid_send, hid_recv,
):
    tok, width = key_grad.shape
    half = width // 2
    quarter = BLOCK // NX
    rep = lax.axis_index("rep")
    me = lax.axis_index("fsdp")
    z, yh, core = me // 4, (me // 2) % 2, me % 2
    yl, x = rep // NX, rep % NX
    mate = (rep, z * 4 + yh * 2 + (1 - core))
    across = (rep, z * 4 + (1 - yh) * 2 + core)
    up = (rep, lax.rem(z + 1, NZ) * 4 + yh * 2 + core)
    down = (rep, lax.rem(z + NZ - 1, NZ) * 4 + yh * 2 + core)
    toward = {1: up, -1: down}
    beside = ((1 - yl) * NX + x, me)
    along = {e: (yl * NX + lax.rem(x + e, NX), me) for e in range(1, NX)}
    rows_a, rows_b = pl.ds(0, ROWS_A), pl.ds(ROWS_A, ROWS_B)
    cols = {1: pl.ds(0, half), -1: pl.ds(half, half)}
    copies = {}

    def block_cols(q, c):
        d, p = distance(q // 2), q % 2
        zz = lax.rem(z + d + 2 * NZ, NZ)
        yy = lax.rem(yh + p, 2)
        return pl.ds(pl.multiple_of((zz * 4 + yy * 2 + c) * BLOCK, BLOCK), BLOCK)

    def hidden_local(q):
        return pltpu.make_async_copy(
            hidden.at[:, block_cols(q, core)], held.at[q, pl.ds(0, tok)], local_sem.at[q]
        )

    def hidden_remote(q):
        return pltpu.make_async_remote_copy(
            src_ref=hidden.at[:, block_cols(q, 1 - core)],
            dst_ref=held.at[q, pl.ds(tok, tok)],
            send_sem=hid_send.at[q],
            recv_sem=hid_recv.at[q],
            device_id=mate,
            device_id_type=MESH,
        )

    def send(name, src, dst, target):
        index = len(copies)
        copies[name] = pltpu.make_async_remote_copy(
            src_ref=src,
            dst_ref=dst,
            send_sem=send_sem.at[index],
            recv_sem=recv_sem.at[index],
            device_id=target,
            device_id_type=MESH,
        )
        copies[name].start()

    def arrived(name):
        copies[name].wait_recv()

    def loop_rows(count, body):
        @pl.loop(0, count // STEP)
        def _(i):
            body(pl.multiple_of(i * STEP, STEP))

    loads = [
        pltpu.make_async_copy(src, dst, raw_sem.at[i])
        for i, (src, dst) in enumerate(((weights, raw_weights), (anchor, raw_anchor), (key_grad, raw_grad), (tokens, raw_tokens)))
    ]
    for load in loads:
        load.start()

    @pl.loop(0, 16)
    def _(q):
        hidden_local(q).start()

    barrier = pltpu.get_barrier_semaphore()
    partners = (mate, across, up, down, beside, *along.values())
    for target in partners:
        pl.semaphore_signal(barrier, inc=1, device_id=target, device_id_type=MESH)
    own = slot(0, 0)
    loads[0].wait()

    def cast(r):
        wire[own, pl.ds(r, STEP)] = raw_weights[pl.ds(r, STEP)].astype(BF16)

    loop_rows(BLOCK, cast)
    loads[1].wait()
    in_second = fragment[0].astype(F32)

    def subtract(r):
        at = pl.ds(r, STEP)
        gap = raw_anchor[at] - raw_weights[at]
        differ[at] = gap[:, :half] * (1.0 - in_second) + gap[:, half:] * in_second

    loop_rows(BLOCK, subtract)
    loads[2].wait()
    loads[3].wait()
    live = (raw_tokens[...] != 0).astype(F32)
    live_rows = jnp.transpose(jnp.broadcast_to(live, (128, tok))).astype(BF16)
    for j in range(width // 128):
        at = pl.ds(j * 128, 128)
        grads_in[pl.ds(0, tok), at] = raw_grad[:, at] * live_rows
    count_pair[...] = jnp.broadcast_to(jnp.sum(live, axis=1, keepdims=True), count_pair.shape)
    pl.semaphore_wait(barrier, len(partners))

    send("ay0", wire.at[own, rows_a], wire.at[slot(0, 1), rows_a], across)
    for s in (1, -1):
        send(("az", s, 1, 0), wire.at[own], wire.at[slot(-s, 0)], toward[s])
    send("ayB0", wire.at[own, rows_b], wire.at[slot(0, 1), rows_b], across)
    send("count_mate", count_pair, count_mate, mate)
    send("mask", grads_in.at[pl.ds(0, tok)], grads_in.at[pl.ds(tok, tok)], mate)

    @pl.loop(0, 16)
    def _(q):
        hidden_remote(q).start()

    for e in range(1, NX):
        at = pl.ds(pl.multiple_of(lax.rem(x + e, NX) * quarter, quarter), quarter)
        send(("dx", e), differ.at[at], from_x.at[e - 1], along[e])
    own_quarter = pl.ds(pl.multiple_of(x * quarter, quarter), quarter)

    def difference_x():
        for e in range(1, NX):
            arrived(("dx", e))
        piece[...] = differ[own_quarter] + from_x[0] + from_x[1] + from_x[2]
        send("dy", piece, from_y, beside)

    def difference_y():
        arrived("dy")
        delta[own_quarter] = (piece[...] + from_y[...]) * (1.0 / 8.0)
        for e in range(1, NX):
            send(("dg", e), delta.at[own_quarter], delta.at[own_quarter], along[e])

    def count_chip():
        arrived("count_mate")
        counts[0] = count_pair[...] + count_mate[...]
        send("count_across", counts.at[0], count_across, across)

    def count_column():
        arrived("count_across")
        counts[1] = counts[0] + count_across[...]
        for s in (1, -1):
            send(("cz", s, 1), counts.at[1], counts.at[1 + (-s) % NZ], toward[s])

    def count_hop(k):
        for s in (1, -1):
            arrived(("cz", s, k - 1))
            if k < 4 or s == 1:
                send(("cz", s, k), counts.at[1 + (-s * (k - 1)) % NZ], counts.at[1 + (-s * k) % NZ], toward[s])

    def gather_hop(k, p):
        for s in (1, -1):
            src = slot(-s * (k - 1), p)
            dst = slot(4 if k == 4 else -s * k, p)
            rows = pl.ds(0, BLOCK) if p == 0 else rows_a
            if k > 1:
                arrived(("az", s, k - 1, p))
            if k == 4:
                send(("az", s, k, p), wire.at[src, rows, cols[s]], wire.at[dst, rows, cols[s]], toward[s])
            else:
                send(("az", s, k, p), wire.at[src, rows], wire.at[dst, rows], toward[s])
            if p == 0 and k > 1:
                send(("ayB", src), wire.at[src, rows_b], wire.at[src + 1, rows_b], across)

    def gather_step(k):
        gather_hop(k, 0)
        gather_hop(k, 1)

    def gradient(*distances):
        first = order(distances[0])

        @pl.loop(2 * first, 2 * (first + len(distances)))
        def _(q):
            hidden_local(q).wait()
            hidden_remote(q).wait_recv()
            parts[q] = lax.dot_general(
                held[q], grads_in[...], (((0,), (0,)), ((), ())), preferred_element_type=F32
            )

        for d in distances:
            o = order(d)

            def stage(r, o=o):
                send_y[o, pl.ds(r, STEP)] = parts[2 * o + 1, pl.ds(ROWS_A + r, STEP)].astype(BF16)

            loop_rows(ROWS_B, stage)
            send(("ry", d), send_y.at[o], recv_y.at[o], across)

    def reduce_far(p):
        for s in (1, -1):
            def stage(r, s=s):
                here = parts[slot(4, p), pl.ds(r, STEP), cols[s]]
                send_z[0 if s == 1 else 1, 3, pl.ds(p * BLOCK + r, STEP), cols[s]] = here.astype(BF16)

            def stage_b(r, s=s):
                here = parts[slot(4, p), pl.ds(ROWS_A + r, STEP), cols[s]]
                here = here + recv_y[order(4), pl.ds(r, STEP), cols[s]].astype(F32)
                send_z[0 if s == 1 else 1, 3, pl.ds(ROWS_A + r, STEP), cols[s]] = here.astype(BF16)

            loop_rows(ROWS_A, stage)
            if p == 0:
                if s == 1:
                    arrived(("ry", 4))
                loop_rows(ROWS_B, stage_b)
            rows = pl.ds(0, BLOCK) if p == 0 else pl.ds(BLOCK, ROWS_A)
            w = 0 if s == 1 else 1
            send(("rz", s, 4, p), send_z.at[w, 3, rows, cols[s]], recv_z.at[w, 3, rows, cols[s]], toward[s])

    def reduce_hop(d, p):
        for s in (1, -1):
            w = 0 if s == 1 else 1
            arrived(("rz", s, d + 1, p))
            if p == 0:
                arrived(("ry", s * d))

            def put(r, base, with_y, s=s, w=w):
                here = parts[slot(s * d, p), pl.ds(base + r, STEP)]
                at = pl.ds(p * BLOCK + base + r, STEP)
                if with_y:
                    here = here + recv_y[order(s * d), pl.ds(r, STEP)].astype(F32)
                if d == 3:
                    lo = 0 if s == 1 else half
                    there = recv_z[w, d, at, cols[s]].astype(F32)
                    summed = here[:, lo:lo + half] + there
                    send_z[w, d - 1, at, cols[s]] = summed.astype(BF16)
                    send_z[w, d - 1, at, cols[-s]] = here[:, half - lo:2 * half - lo].astype(BF16)
                else:
                    there = recv_z[w, d, at].astype(F32)
                    send_z[w, d - 1, at] = (here + there).astype(BF16)

            loop_rows(ROWS_A, lambda r: put(r, 0, False))
            if p == 0:
                loop_rows(ROWS_B, lambda r: put(r, ROWS_A, True))
            rows = pl.ds(0, BLOCK) if p == 0 else pl.ds(BLOCK, ROWS_A)
            send(("rz", s, d, p), send_z.at[w, d - 1, rows], recv_z.at[w, d - 1, rows], toward[s])

    def keys(*distances):
        for d in distances:
            q = slot(d, 0)
            if d == 0:
                arrived("ayB0")
            elif d == 4:
                arrived(("ayB", 4, 1))
                arrived(("ayB", 4, -1))
            else:
                arrived(("ayB", q))
            acc[...] += jnp.dot(held[q], wire[q], preferred_element_type=F32) + jnp.dot(
                held[q + 1], wire[q + 1], preferred_element_type=F32
            )

    arrived("mask")
    gradient(4)
    reduce_far(1)
    arrived("ay0")
    gather_hop(1, 1)
    count_chip()
    gradient(3, -3)
    reduce_far(0)
    gather_step(2)
    difference_x()
    count_column()
    gradient(2, -2)
    reduce_hop(3, 1)
    reduce_hop(3, 0)
    gather_step(3)
    count_hop(2)
    difference_y()
    gradient(1, -1, 0)
    acc[...] = jnp.zeros_like(acc)
    reduce_hop(2, 1)
    reduce_hop(2, 0)
    gather_step(4)
    count_hop(3)
    keys(0)
    reduce_hop(1, 1)
    reduce_hop(1, 0)
    count_hop(4)
    for s in (1, -1):
        arrived(("az", s, 4, 0))
        src = slot(4, 0)
        send(("ayB", 4, s), wire.at[src, rows_b, cols[s]], wire.at[src + 1, rows_b, cols[s]], across)
    keys(1, -1, 2, -2, 3, -3)
    arrived(("cz", 1, 4))
    group_count = counts[1]
    for i in range(1, NZ):
        group_count = group_count + counts[1 + i]
    scale = ((1.0 / math.sqrt(D)) / group_count)[0:1, 0:1]
    for e in range(1, NX):
        arrived(("dg", e))
    delta_out[...] = delta[...]

    for s in (1, -1):
        arrived(("rz", s, 1, 1))

    def close_a(r):
        at = pl.ds(BLOCK + r, STEP)
        total = parts[slot(0, 1), pl.ds(r, STEP)] + recv_z[0, 0, at].astype(F32) + recv_z[1, 0, at].astype(F32)
        send_a[pl.ds(r, STEP)] = total.astype(BF16)

    loop_rows(ROWS_A, close_a)
    send("rya", send_a, recv_a, across)
    for s in (1, -1):
        arrived(("az", s, 4, 1))
    keys(4)
    send("keys", acc.at[pl.ds(tok, tok)], other, mate)
    for s in (1, -1):
        arrived(("rz", s, 1, 0))
    arrived(("ry", 0))

    def close_b(r):
        at = pl.ds(ROWS_A + r, STEP)
        total = parts[slot(0, 0), at] + recv_y[order(0), pl.ds(r, STEP)].astype(F32)
        grad_out[at] = (total + recv_z[0, 0, at].astype(F32) + recv_z[1, 0, at].astype(F32)) * scale

    loop_rows(ROWS_B, close_b)
    arrived("rya")

    def close_all(r):
        at = pl.ds(r, STEP)
        total = parts[slot(0, 0), at] + recv_a[at].astype(F32)
        grad_out[at] = (total + recv_z[0, 0, at].astype(F32) + recv_z[1, 0, at].astype(F32)) * scale

    loop_rows(ROWS_A, close_all)
    arrived("keys")

    def close_keys(r):
        at = pl.ds(r, STEP)
        keys_out[at] = ((acc[at] + other[at]) * (1.0 / math.sqrt(D))).astype(BF16)

    loop_rows(tok, close_keys)
    for copy in copies.values():
        copy.wait_send()

    @pl.loop(0, 16)
    def _(q):
        hidden_remote(q).wait_send()


def exchange(hidden, tokens, key_grad, weights, anchor, fragment):
    tok, width = key_grad.shape
    half = width // 2
    vmem = pl.BlockSpec(memory_space=pltpu.VMEM)
    smem = pl.BlockSpec(memory_space=pltpu.SMEM)
    anywhere = pl.BlockSpec(memory_space=pl.ANY)
    hbm = pl.BlockSpec(memory_space=pltpu.HBM)
    count = 96
    tile = pltpu.VMEM((8, 128), F32)
    return pl.pallas_call(
        kernel,
        out_shape=(
            jax.ShapeDtypeStruct((BLOCK, width), F32),
            jax.ShapeDtypeStruct((tok, width), BF16),
            jax.ShapeDtypeStruct((BLOCK, half), F32),
        ),
        in_specs=[hbm] * 5 + [smem],
        out_specs=(vmem, vmem, vmem),
        scratch_shapes=[
            pltpu.VMEM((16, 2 * tok, BLOCK), BF16),
            pltpu.VMEM((2 * tok, width), BF16),
            pltpu.VMEM((16, BLOCK, width), F32),
            pltpu.VMEM((16, BLOCK, width), BF16),
            pltpu.VMEM((2 * tok, width), F32),
            pltpu.VMEM((tok, width), F32),
            pltpu.VMEM((2, 4, BLOCK + ROWS_A, width), BF16),
            pltpu.VMEM((2, 4, BLOCK + ROWS_A, width), BF16),
            pltpu.VMEM((8, ROWS_B, width), BF16),
            pltpu.VMEM((8, ROWS_B, width), BF16),
            pltpu.VMEM((ROWS_A, width), BF16),
            pltpu.VMEM((ROWS_A, width), BF16),
            pltpu.VMEM((tok, width), BF16),
            pltpu.VMEM((BLOCK, width), F32),
            pltpu.VMEM((BLOCK, width), F32),
            pltpu.VMEM(tokens.shape, jnp.int32),
            pltpu.VMEM((BLOCK, half), F32),
            pltpu.VMEM((NX - 1, BLOCK // NX, half), F32),
            pltpu.VMEM((BLOCK // NX, half), F32),
            pltpu.VMEM((BLOCK // NX, half), F32),
            pltpu.VMEM((BLOCK, half), F32),
            pltpu.VMEM((1 + NZ, 8, 128), F32),
            tile,
            tile,
            tile,
            pltpu.SemaphoreType.DMA((16,)),
            pltpu.SemaphoreType.DMA((4,)),
            pltpu.SemaphoreType.DMA((count,)),
            pltpu.SemaphoreType.DMA((count,)),
            pltpu.SemaphoreType.DMA((16,)),
            pltpu.SemaphoreType.DMA((16,)),
        ],
        compiler_params=pltpu.CompilerParams(
            collective_id=0, has_side_effects=True, vmem_limit_bytes=52 * 2**20
        ),
        cost_estimate=pl.CostEstimate(flops=13 * 10**9, bytes_accessed=16 * 2**20, transcendentals=0),
    )(hidden, tokens, key_grad, weights, anchor, fragment)


def finish_kernel(
    grad, delta, keys, first, second, weights, anchor, momentum, fragment, step_count,
    keys_out, weights_out, first_out, second_out, anchor_out, momentum_out,
    new_weights, new_first, new_second, new_anchor, new_momentum, sems,
):
    rows, width = grad.shape
    half = width // 2
    part = rows // FINISH_PARTS
    writes = [pltpu.make_async_copy(keys, keys_out, sems.at[0])]
    writes[0].start()

    def write(src, dst, at):
        writes.append(pltpu.make_async_copy(src.at[at], dst.at[at], sems.at[len(writes)]))
        writes[-1].start()

    steps = jnp.full((1, half), step_count[0], jnp.int32).astype(F32)
    first_scale = 1.0 / (1.0 - jnp.exp(steps * math.log(BETA_ONE)))
    second_scale = 1.0 / (1.0 - jnp.exp(steps * math.log(BETA_TWO)))
    for i in range(FINISH_PARTS):
        at = pl.ds(i * part, part)
        gap = delta[at]
        for h in range(FRAGS):
            cols = pl.ds(h * half, half)
            moved = fragment[0] == h
            old_anchor, old_momentum = anchor[at, cols], momentum[at, cols]
            moved_momentum = OUTER_MOMENTUM * old_momentum + gap
            moved_anchor = old_anchor - OUTER_LR * (gap + OUTER_MOMENTUM * moved_momentum)
            new_momentum[at, cols] = jnp.where(moved, moved_momentum, old_momentum)
            new_anchor[at, cols] = jnp.where(moved, moved_anchor, old_anchor)
            gradient = grad[at, cols]
            one = BETA_ONE * first[at, cols] + (1.0 - BETA_ONE) * gradient
            two = BETA_TWO * second[at, cols] + (1.0 - BETA_TWO) * gradient * gradient
            new_first[at, cols] = one
            new_second[at, cols] = two
            ratio = one * first_scale / (jnp.sqrt(two * second_scale) + EPSILON)
            old = weights[at, cols]
            stepped = old - INNER_LR * (ratio + WEIGHT_DECAY * old)
            mixed = MIX_LOCAL * stepped + (1.0 - MIX_LOCAL) * moved_anchor
            new_weights[at, cols] = jnp.where(moved, mixed, stepped)
        write(new_momentum, momentum_out, at)
        write(new_anchor, anchor_out, at)
        write(new_first, first_out, at)
        write(new_second, second_out, at)
        write(new_weights, weights_out, at)
    for copy in writes:
        copy.wait()


FINISH_PARTS = 4


def finish(grad, delta, keys, first, second, weights, anchor, momentum, fragment, step_count):
    vmem = pl.BlockSpec(memory_space=pltpu.VMEM)
    smem = pl.BlockSpec(memory_space=pltpu.SMEM)
    anywhere = pl.BlockSpec(memory_space=pl.ANY)
    block = jax.ShapeDtypeStruct(grad.shape, F32)
    return pl.pallas_call(
        finish_kernel,
        out_shape=(jax.ShapeDtypeStruct(keys.shape, keys.dtype),) + (block,) * 5,
        in_specs=[vmem, vmem, anywhere] + [vmem] * 5 + [smem, smem],
        out_specs=(anywhere,) * 6,
        scratch_shapes=[pltpu.VMEM(grad.shape, F32)] * 5 + [pltpu.SemaphoreType.DMA((1 + 5 * FINISH_PARTS,))],
        compiler_params=pltpu.CompilerParams(vmem_limit_bytes=16 * 2**20),
    )(grad, delta, keys, first, second, weights, anchor, momentum, fragment, step_count)


def on_device(
    hidden,
    token_ids,
    key_grad,
    weights,
    first_moment,
    second_moment,
    anchor,
    momentum,
    fragment,
    step_count,
):
    grad, keys, delta = exchange(hidden[0], token_ids, key_grad[0], weights[0], anchor, fragment)
    keys, new_weights, new_first, new_second, new_anchor, new_momentum = finish(
        grad, delta, keys, first_moment[0], second_moment[0], weights[0], anchor, momentum, fragment, step_count
    )
    return keys[None], new_weights[None], new_first[None], new_second[None], new_anchor, new_momentum


def solution(mesh):
    return jax.shard_map(
        on_device,
        mesh=mesh,
        in_specs=(
            P("rep", "fsdp", None),
            P("rep", "fsdp"),
            P("rep", "fsdp", None),
            P("rep", "fsdp", None),
            P("rep", "fsdp", None),
            P("rep", "fsdp", None),
            P("fsdp", None),
            P("fsdp", None),
            P(),
            P(),
        ),
        out_specs=(
            P("rep", "fsdp", None),
            P("rep", "fsdp", None),
            P("rep", "fsdp", None),
            P("rep", "fsdp", None),
            P("fsdp", None),
            P("fsdp", None),
        ),
        check_vma=False,
    )
```

```python
import math

import jax
import jax.numpy as jnp
from jax import lax
from jax.experimental import pallas as pl
from jax.experimental.pallas import tpu as pltpu
from jax.sharding import PartitionSpec as P

MESH = pl.DeviceIdType.MESH
BF16, F32 = jnp.bfloat16, jnp.float32

D = 8192
FRAGS = 2
NZ = 8
NX = 4
BLOCK = 256
ROWS_A = 112
ROWS_B = BLOCK - ROWS_A
STEP = 16

BETA_ONE = 0.9
BETA_TWO = 0.95
EPSILON = 1e-08
INNER_LR = 0.1
WEIGHT_DECAY = 0.1
OUTER_LR = 0.7
OUTER_MOMENTUM = 0.9
MIX_LOCAL = 0.5


def order(d):
    return {4: 0, 3: 1, -3: 2, 2: 3, -2: 4, 1: 5, -1: 6, 0: 7}[d]


def slot(d, p):
    return 2 * order(d) + p


def distance(o):
    far = 4 - (o + 1) // 2
    return jnp.where(o % 2 == 1, far, -far)


def kernel(
    hidden, tokens, key_grad, weights, anchor, fragment, grad_out, keys_out, delta_out,
    held, grads_in, parts, wire, acc, other, send_z, recv_z, send_y, recv_y, send_a, recv_a,
    raw_grad, raw_weights, raw_anchor, raw_tokens, differ, from_x, piece, from_y, delta, counts, count_mate, count_pair, count_across, count_total,
    local_sem, raw_sem, send_sem, recv_sem, hid_send, hid_recv,
):
    tok, width = key_grad.shape
    half = width // 2
    quarter = BLOCK // NX
    rep = lax.axis_index("rep")
    me = lax.axis_index("fsdp")
    z, yh, core = me // 4, (me // 2) % 2, me % 2
    yl, x = rep // NX, rep % NX
    mate = (rep, z * 4 + yh * 2 + (1 - core))
    across = (rep, z * 4 + (1 - yh) * 2 + core)
    up = (rep, lax.rem(z + 1, NZ) * 4 + yh * 2 + core)
    down = (rep, lax.rem(z + NZ - 1, NZ) * 4 + yh * 2 + core)
    toward = {1: up, -1: down}
    beside = ((1 - yl) * NX + x, me)
    along = {e: (yl * NX + lax.rem(x + e, NX), me) for e in range(1, NX)}
    rows_a, rows_b = pl.ds(0, ROWS_A), pl.ds(ROWS_A, ROWS_B)
    cols = {1: pl.ds(0, half), -1: pl.ds(half, half)}
    copies = {}

    def block_cols(q, c):
        d, p = distance(q // 2), q % 2
        zz = lax.rem(z + d + 2 * NZ, NZ)
        yy = lax.rem(yh + p, 2)
        return pl.ds(pl.multiple_of((zz * 4 + yy * 2 + c) * BLOCK, BLOCK), BLOCK)

    def hidden_local(q):
        return pltpu.make_async_copy(
            hidden.at[:, block_cols(q, core)], held.at[q, pl.ds(0, tok)], local_sem.at[q]
        )

    def hidden_remote(q):
        return pltpu.make_async_remote_copy(
            src_ref=hidden.at[:, block_cols(q, 1 - core)],
            dst_ref=held.at[q, pl.ds(tok, tok)],
            send_sem=hid_send.at[q],
            recv_sem=hid_recv.at[q],
            device_id=mate,
            device_id_type=MESH,
        )

    def send(name, src, dst, target):
        index = len(copies)
        copies[name] = pltpu.make_async_remote_copy(
            src_ref=src,
            dst_ref=dst,
            send_sem=send_sem.at[index],
            recv_sem=recv_sem.at[index],
            device_id=target,
            device_id_type=MESH,
        )
        copies[name].start()

    def arrived(name):
        copies[name].wait_recv()

    def loop_rows(count, body):
        @pl.loop(0, count // STEP)
        def _(i):
            body(pl.multiple_of(i * STEP, STEP))

    loads = [
        pltpu.make_async_copy(src, dst, raw_sem.at[i])
        for i, (src, dst) in enumerate(((weights, raw_weights), (anchor, raw_anchor), (key_grad, raw_grad), (tokens, raw_tokens)))
    ]
    for load in loads:
        load.start()

    @pl.loop(0, 16)
    def _(q):
        hidden_local(q).start()

    barrier = pltpu.get_barrier_semaphore()
    partners = (mate, across, up, down, beside, *along.values())
    for target in partners:
        pl.semaphore_signal(barrier, inc=1, device_id=target, device_id_type=MESH)
    own = slot(0, 0)
    loads[0].wait()

    def cast(r):
        wire[own, pl.ds(r, STEP)] = raw_weights[pl.ds(r, STEP)].astype(BF16)

    loop_rows(BLOCK, cast)
    pl.semaphore_wait(barrier, len(partners))

    send("ay0", wire.at[own, rows_a], wire.at[slot(0, 1), rows_a], across)
    for s in (1, -1):
        send(("az", s, 1, 0), wire.at[own], wire.at[slot(-s, 0)], toward[s])

    @pl.loop(0, 2)
    def _(q):
        hidden_remote(q).start()

    loads[2].wait()
    loads[3].wait()
    live = (raw_tokens[...] != 0).astype(F32)
    live_rows = jnp.transpose(jnp.broadcast_to(live, (128, tok))).astype(BF16)
    for j in range(width // 128):
        at = pl.ds(j * 128, 128)
        grads_in[pl.ds(0, tok), at] = raw_grad[:, at] * live_rows
    count_pair[...] = jnp.broadcast_to(jnp.sum(live, axis=1, keepdims=True), count_pair.shape)
    send("count_mate", count_pair, count_mate, mate)
    send("mask", grads_in.at[pl.ds(0, tok)], grads_in.at[pl.ds(tok, tok)], mate)

    @pl.loop(2, 16)
    def _(q):
        hidden_remote(q).start()

    loads[1].wait()
    in_second = fragment[0].astype(F32)

    def subtract(r):
        at = pl.ds(r, STEP)
        gap = raw_anchor[at] - raw_weights[at]
        differ[at] = gap[:, :half] * (1.0 - in_second) + gap[:, half:] * in_second

    loop_rows(BLOCK, subtract)

    for e in range(1, NX):
        at = pl.ds(pl.multiple_of(lax.rem(x + e, NX) * quarter, quarter), quarter)
        send(("dx", e), differ.at[at], from_x.at[e - 1], along[e])
    own_quarter = pl.ds(pl.multiple_of(x * quarter, quarter), quarter)

    def difference_x():
        for e in range(1, NX):
            arrived(("dx", e))
        piece[...] = differ[own_quarter] + from_x[0] + from_x[1] + from_x[2]
        send("dy", piece, from_y, beside)

    def difference_y():
        arrived("dy")
        delta[own_quarter] = (piece[...] + from_y[...]) * (1.0 / 8.0)
        for e in range(1, NX):
            send(("dg", e), delta.at[own_quarter], delta.at[own_quarter], along[e])

    def count_hop(k):
        if k == 1:
            arrived("count_mate")
            counts[0] = count_pair[...] + count_mate[...]
        for s in (1, -1):
            if k > 1:
                arrived(("cz", s, k - 1))
            if k < 4 or s == 1:
                send(("cz", s, k), counts.at[(-s * (k - 1)) % NZ], counts.at[(-s * k) % NZ], toward[s])

    def count_column():
        arrived(("cz", 1, 4))
        total = counts[0]
        for i in range(1, NZ):
            total = total + counts[i]
        count_total[...] = total
        send("count_across", count_total, count_across, across)

    def gather_hop(k, p):
        for s in (1, -1):
            src = slot(-s * (k - 1), p)
            dst = slot(4 if k == 4 else -s * k, p)
            rows = pl.ds(0, BLOCK) if p == 0 else rows_a
            if k > 1:
                arrived(("az", s, k - 1, p))
            if k == 4:
                send(("az", s, k, p), wire.at[src, rows, cols[s]], wire.at[dst, rows, cols[s]], toward[s])
            else:
                send(("az", s, k, p), wire.at[src, rows], wire.at[dst, rows], toward[s])
            if p == 0 and k > 1:
                send(("ayB", src), wire.at[src, rows_b], wire.at[src + 1, rows_b], across)

    def gather_step(k):
        count_hop(k)
        gather_hop(k, 0)
        gather_hop(k, 1)

    def gradient(*distances):
        first = order(distances[0])

        @pl.loop(2 * first, 2 * (first + len(distances)))
        def _(q):
            hidden_local(q).wait()
            hidden_remote(q).wait_recv()
            parts[q] = lax.dot_general(
                held[q], grads_in[...], (((0,), (0,)), ((), ())), preferred_element_type=F32
            )

        for d in distances:
            o = order(d)

            def stage(r, o=o):
                send_y[o, pl.ds(r, STEP)] = parts[2 * o + 1, pl.ds(ROWS_A + r, STEP)].astype(BF16)

            loop_rows(ROWS_B, stage)

    def part_y(*distances):
        for d in distances:
            send(("ry", d), send_y.at[order(d)], recv_y.at[order(d)], across)

    def reduce_far(p):
        for s in (1, -1):
            def stage(r, s=s):
                here = parts[slot(4, p), pl.ds(r, STEP), cols[s]]
                send_z[0 if s == 1 else 1, 3, pl.ds(p * BLOCK + r, STEP), cols[s]] = here.astype(BF16)

            def stage_b(r, s=s):
                here = parts[slot(4, p), pl.ds(ROWS_A + r, STEP), cols[s]]
                here = here + recv_y[order(4), pl.ds(r, STEP), cols[s]].astype(F32)
                send_z[0 if s == 1 else 1, 3, pl.ds(ROWS_A + r, STEP), cols[s]] = here.astype(BF16)

            loop_rows(ROWS_A, stage)
            if p == 0:
                if s == 1:
                    arrived(("ry", 4))
                loop_rows(ROWS_B, stage_b)
            rows = pl.ds(0, BLOCK) if p == 0 else pl.ds(BLOCK, ROWS_A)
            w = 0 if s == 1 else 1
            send(("rz", s, 4, p), send_z.at[w, 3, rows, cols[s]], recv_z.at[w, 3, rows, cols[s]], toward[s])

    def reduce_hop(d, p):
        for s in (1, -1):
            w = 0 if s == 1 else 1
            arrived(("rz", s, d + 1, p))
            if p == 0:
                arrived(("ry", s * d))

            def put(r, base, with_y, s=s, w=w):
                here = parts[slot(s * d, p), pl.ds(base + r, STEP)]
                at = pl.ds(p * BLOCK + base + r, STEP)
                if with_y:
                    here = here + recv_y[order(s * d), pl.ds(r, STEP)].astype(F32)
                if d == 3:
                    lo = 0 if s == 1 else half
                    there = recv_z[w, d, at, cols[s]].astype(F32)
                    summed = here[:, lo:lo + half] + there
                    send_z[w, d - 1, at, cols[s]] = summed.astype(BF16)
                    send_z[w, d - 1, at, cols[-s]] = here[:, half - lo:2 * half - lo].astype(BF16)
                else:
                    there = recv_z[w, d, at].astype(F32)
                    send_z[w, d - 1, at] = (here + there).astype(BF16)

            loop_rows(ROWS_A, lambda r: put(r, 0, False))
            if p == 0:
                loop_rows(ROWS_B, lambda r: put(r, ROWS_A, True))
            rows = pl.ds(0, BLOCK) if p == 0 else pl.ds(BLOCK, ROWS_A)
            send(("rz", s, d, p), send_z.at[w, d - 1, rows], recv_z.at[w, d - 1, rows], toward[s])

    def keys(*distances):
        for d in distances:
            q = slot(d, 0)
            if d == 0:
                arrived("ayB0")
            elif d == 4:
                arrived(("ayB", 4, 1))
                arrived(("ayB", 4, -1))
            else:
                arrived(("ayB", q))
            acc[...] += jnp.dot(held[q], wire[q], preferred_element_type=F32) + jnp.dot(
                held[q + 1], wire[q + 1], preferred_element_type=F32
            )

    arrived("mask")
    gradient(4)
    part_y(4)
    reduce_far(1)
    count_hop(1)
    arrived("ay0")
    gather_hop(1, 1)
    send("ayB0", wire.at[own, rows_b], wire.at[slot(0, 1), rows_b], across)
    gradient(3, -3)
    part_y(3, -3)
    count_hop(2)
    gather_hop(2, 0)
    reduce_far(0)
    gather_hop(2, 1)
    difference_x()
    gradient(2, -2)
    part_y(2, -2)
    reduce_hop(3, 1)
    reduce_hop(3, 0)
    gather_step(3)
    difference_y()
    gradient(1, -1, 0)
    part_y(1, -1)
    acc[...] = jnp.zeros_like(acc)
    reduce_hop(2, 1)
    reduce_hop(2, 0)
    gather_step(4)
    part_y(0)
    keys(0)
    reduce_hop(1, 1)
    reduce_hop(1, 0)
    count_column()
    for s in (1, -1):
        arrived(("az", s, 4, 0))
        src = slot(4, 0)
        send(("ayB", 4, s), wire.at[src, rows_b, cols[s]], wire.at[src + 1, rows_b, cols[s]], across)
    keys(1, -1, 2, -2, 3, -3)
    for e in range(1, NX):
        arrived(("dg", e))
    delta_out[...] = delta[...]

    for s in (1, -1):
        arrived(("rz", s, 1, 1))

    def close_a(r):
        at = pl.ds(BLOCK + r, STEP)
        total = parts[slot(0, 1), pl.ds(r, STEP)] + recv_z[0, 0, at].astype(F32) + recv_z[1, 0, at].astype(F32)
        send_a[pl.ds(r, STEP)] = total.astype(BF16)

    loop_rows(ROWS_A, close_a)
    send("rya", send_a, recv_a, across)
    for s in (1, -1):
        arrived(("az", s, 4, 1))
    arrived("count_across")
    scale = ((1.0 / math.sqrt(D)) / (count_total[...] + count_across[...]))[0:1, 0:1]
    keys(4)
    send("keys", acc.at[pl.ds(tok, tok)], other, mate)
    for s in (1, -1):
        arrived(("rz", s, 1, 0))
    arrived(("ry", 0))

    def close_b(r):
        at = pl.ds(ROWS_A + r, STEP)
        total = parts[slot(0, 0), at] + recv_y[order(0), pl.ds(r, STEP)].astype(F32)
        grad_out[at] = (total + recv_z[0, 0, at].astype(F32) + recv_z[1, 0, at].astype(F32)) * scale

    loop_rows(ROWS_B, close_b)
    arrived("rya")

    def close_all(r):
        at = pl.ds(r, STEP)
        total = parts[slot(0, 0), at] + recv_a[at].astype(F32)
        grad_out[at] = (total + recv_z[0, 0, at].astype(F32) + recv_z[1, 0, at].astype(F32)) * scale

    loop_rows(ROWS_A, close_all)
    arrived("keys")

    def close_keys(r):
        at = pl.ds(r, STEP)
        keys_out[at] = ((acc[at] + other[at]) * (1.0 / math.sqrt(D))).astype(BF16)

    loop_rows(tok, close_keys)
    for copy in copies.values():
        copy.wait_send()

    @pl.loop(0, 16)
    def _(q):
        hidden_remote(q).wait_send()


def exchange(hidden, tokens, key_grad, weights, anchor, fragment):
    tok, width = key_grad.shape
    half = width // 2
    vmem = pl.BlockSpec(memory_space=pltpu.VMEM)
    smem = pl.BlockSpec(memory_space=pltpu.SMEM)
    anywhere = pl.BlockSpec(memory_space=pl.ANY)
    hbm = pl.BlockSpec(memory_space=pltpu.HBM)
    count = 96
    tile = pltpu.VMEM((8, 128), F32)
    return pl.pallas_call(
        kernel,
        out_shape=(
            jax.ShapeDtypeStruct((BLOCK, width), F32),
            jax.ShapeDtypeStruct((tok, width), BF16),
            jax.ShapeDtypeStruct((BLOCK, half), F32),
        ),
        in_specs=[hbm] * 5 + [smem],
        out_specs=(vmem, vmem, vmem),
        scratch_shapes=[
            pltpu.VMEM((16, 2 * tok, BLOCK), BF16),
            pltpu.VMEM((2 * tok, width), BF16),
            pltpu.VMEM((16, BLOCK, width), F32),
            pltpu.VMEM((16, BLOCK, width), BF16),
            pltpu.VMEM((2 * tok, width), F32),
            pltpu.VMEM((tok, width), F32),
            pltpu.VMEM((2, 4, BLOCK + ROWS_A, width), BF16),
            pltpu.VMEM((2, 4, BLOCK + ROWS_A, width), BF16),
            pltpu.VMEM((8, ROWS_B, width), BF16),
            pltpu.VMEM((8, ROWS_B, width), BF16),
            pltpu.VMEM((ROWS_A, width), BF16),
            pltpu.VMEM((ROWS_A, width), BF16),
            pltpu.VMEM((tok, width), BF16),
            pltpu.VMEM((BLOCK, width), F32),
            pltpu.VMEM((BLOCK, width), F32),
            pltpu.VMEM(tokens.shape, jnp.int32),
            pltpu.VMEM((BLOCK, half), F32),
            pltpu.VMEM((NX - 1, BLOCK // NX, half), F32),
            pltpu.VMEM((BLOCK // NX, half), F32),
            pltpu.VMEM((BLOCK // NX, half), F32),
            pltpu.VMEM((BLOCK, half), F32),
            pltpu.VMEM((NZ, 8, 128), F32),
            tile,
            tile,
            tile,
            tile,
            pltpu.SemaphoreType.DMA((16,)),
            pltpu.SemaphoreType.DMA((4,)),
            pltpu.SemaphoreType.DMA((count,)),
            pltpu.SemaphoreType.DMA((count,)),
            pltpu.SemaphoreType.DMA((16,)),
            pltpu.SemaphoreType.DMA((16,)),
        ],
        compiler_params=pltpu.CompilerParams(
            collective_id=0, has_side_effects=True, vmem_limit_bytes=46 * 2**20
        ),
        cost_estimate=pl.CostEstimate(flops=13 * 10**9, bytes_accessed=16 * 2**20, transcendentals=0),
    )(hidden, tokens, key_grad, weights, anchor, fragment)


def finish_kernel(
    grad, delta, keys, first, second, weights, anchor, momentum, fragment, step_count,
    keys_out, weights_out, first_out, second_out, anchor_out, momentum_out,
    new_weights, new_first, new_second, new_anchor, new_momentum, sems,
):
    rows, width = grad.shape
    half = width // 2
    part = rows // FINISH_PARTS
    writes = [pltpu.make_async_copy(keys, keys_out, sems.at[0])]
    writes[0].start()

    def write(src, dst, at):
        writes.append(pltpu.make_async_copy(src.at[at], dst.at[at], sems.at[len(writes)]))
        writes[-1].start()

    steps = jnp.full((1, half), step_count[0], jnp.int32).astype(F32)
    first_scale = 1.0 / (1.0 - jnp.exp(steps * math.log(BETA_ONE)))
    second_scale = 1.0 / (1.0 - jnp.exp(steps * math.log(BETA_TWO)))
    for i in range(FINISH_PARTS):
        at = pl.ds(i * part, part)
        gap = delta[at]
        for h in range(FRAGS):
            cols = pl.ds(h * half, half)
            moved = fragment[0] == h
            old_anchor, old_momentum = anchor[at, cols], momentum[at, cols]
            moved_momentum = OUTER_MOMENTUM * old_momentum + gap
            moved_anchor = old_anchor - OUTER_LR * (gap + OUTER_MOMENTUM * moved_momentum)
            new_momentum[at, cols] = jnp.where(moved, moved_momentum, old_momentum)
            new_anchor[at, cols] = jnp.where(moved, moved_anchor, old_anchor)
            gradient = grad[at, cols]
            one = BETA_ONE * first[at, cols] + (1.0 - BETA_ONE) * gradient
            two = BETA_TWO * second[at, cols] + (1.0 - BETA_TWO) * gradient * gradient
            new_first[at, cols] = one
            new_second[at, cols] = two
            ratio = one * first_scale / (jnp.sqrt(two * second_scale) + EPSILON)
            old = weights[at, cols]
            stepped = old - INNER_LR * (ratio + WEIGHT_DECAY * old)
            mixed = MIX_LOCAL * stepped + (1.0 - MIX_LOCAL) * moved_anchor
            new_weights[at, cols] = jnp.where(moved, mixed, stepped)
        write(new_momentum, momentum_out, at)
        write(new_anchor, anchor_out, at)
        write(new_first, first_out, at)
        write(new_second, second_out, at)
        write(new_weights, weights_out, at)
    for copy in writes:
        copy.wait()


FINISH_PARTS = 4


def finish(grad, delta, keys, first, second, weights, anchor, momentum, fragment, step_count):
    vmem = pl.BlockSpec(memory_space=pltpu.VMEM)
    smem = pl.BlockSpec(memory_space=pltpu.SMEM)
    anywhere = pl.BlockSpec(memory_space=pl.ANY)
    block = jax.ShapeDtypeStruct(grad.shape, F32)
    return pl.pallas_call(
        finish_kernel,
        out_shape=(jax.ShapeDtypeStruct(keys.shape, keys.dtype),) + (block,) * 5,
        in_specs=[vmem, vmem, anywhere] + [vmem] * 5 + [smem, smem],
        out_specs=(anywhere,) * 6,
        scratch_shapes=[pltpu.VMEM(grad.shape, F32)] * 5 + [pltpu.SemaphoreType.DMA((1 + 5 * FINISH_PARTS,))],
        compiler_params=pltpu.CompilerParams(vmem_limit_bytes=16 * 2**20),
    )(grad, delta, keys, first, second, weights, anchor, momentum, fragment, step_count)


def on_device(
    hidden,
    token_ids,
    key_grad,
    weights,
    first_moment,
    second_moment,
    anchor,
    momentum,
    fragment,
    step_count,
):
    operands = [
        pltpu.with_memory_space_constraint(operand, pltpu.HBM)
        for operand in (hidden[0], token_ids, key_grad[0], weights[0], anchor)
    ]
    grad, keys, delta = exchange(*operands, fragment)
    keys, new_weights, new_first, new_second, new_anchor, new_momentum = finish(
        grad, delta, keys, first_moment[0], second_moment[0], weights[0], anchor, momentum, fragment, step_count
    )
    return keys[None], new_weights[None], new_first[None], new_second[None], new_anchor, new_momentum


def solution(mesh):
    return jax.shard_map(
        on_device,
        mesh=mesh,
        in_specs=(
            P("rep", "fsdp", None),
            P("rep", "fsdp"),
            P("rep", "fsdp", None),
            P("rep", "fsdp", None),
            P("rep", "fsdp", None),
            P("rep", "fsdp", None),
            P("fsdp", None),
            P("fsdp", None),
            P(),
            P(),
        ),
        out_specs=(
            P("rep", "fsdp", None),
            P("rep", "fsdp", None),
            P("rep", "fsdp", None),
            P("rep", "fsdp", None),
            P("fsdp", None),
            P("fsdp", None),
        ),
        check_vma=False,
    )
```

```python
import math

import jax
import jax.numpy as jnp
from jax import lax
from jax.experimental import pallas as pl
from jax.experimental.pallas import tpu as pltpu
from jax.sharding import PartitionSpec as P

MESH = pl.DeviceIdType.MESH
BF16, F32 = jnp.bfloat16, jnp.float32

D = 8192
FRAGS = 2
NZ = 8
NX = 4
BLOCK = 256
ROWS_A = 112
ROWS_B = BLOCK - ROWS_A
STEP = 16

BETA_ONE = 0.9
BETA_TWO = 0.95
EPSILON = 1e-08
INNER_LR = 0.1
WEIGHT_DECAY = 0.1
OUTER_LR = 0.7
OUTER_MOMENTUM = 0.9
MIX_LOCAL = 0.5


def order(d):
    return {4: 0, 3: 1, -3: 2, 2: 3, -2: 4, 1: 5, -1: 6, 0: 7}[d]


def slot(d, p):
    return 2 * order(d) + p


def distance(o):
    far = 4 - (o + 1) // 2
    return jnp.where(o % 2 == 1, far, -far)


def kernel(
    hidden, tokens, key_grad, weights, anchor, fragment, grad_out, keys_out, delta_out,
    held, grads_in, parts, wire, acc, other, send_z, recv_z, send_y, recv_y, send_a, recv_a,
    raw_grad, raw_weights, raw_anchor, raw_tokens, differ, from_x, piece, from_y, delta, counts, count_mate, count_pair, count_across, count_total,
    local_sem, raw_sem, send_sem, recv_sem, hid_send, hid_recv,
):
    tok, width = key_grad.shape
    half = width // 2
    quarter = BLOCK // NX
    rep = lax.axis_index("rep")
    me = lax.axis_index("fsdp")
    z, yh, core = me // 4, (me // 2) % 2, me % 2
    yl, x = rep // NX, rep % NX
    mate = (rep, z * 4 + yh * 2 + (1 - core))
    across = (rep, z * 4 + (1 - yh) * 2 + core)
    up = (rep, lax.rem(z + 1, NZ) * 4 + yh * 2 + core)
    down = (rep, lax.rem(z + NZ - 1, NZ) * 4 + yh * 2 + core)
    toward = {1: up, -1: down}
    beside = ((1 - yl) * NX + x, me)
    along = {e: (yl * NX + lax.rem(x + e, NX), me) for e in range(1, NX)}
    rows_a, rows_b = pl.ds(0, ROWS_A), pl.ds(ROWS_A, ROWS_B)
    cols = {1: pl.ds(0, half), -1: pl.ds(half, half)}
    copies = {}

    def block_cols(q, c):
        d, p = distance(q // 2), q % 2
        zz = lax.rem(z + d + 2 * NZ, NZ)
        yy = lax.rem(yh + p, 2)
        return pl.ds(pl.multiple_of((zz * 4 + yy * 2 + c) * BLOCK, BLOCK), BLOCK)

    def hidden_local(q):
        return pltpu.make_async_copy(
            hidden.at[:, block_cols(q, core)], held.at[q, pl.ds(0, tok)], local_sem.at[q]
        )

    def hidden_remote(q):
        return pltpu.make_async_remote_copy(
            src_ref=hidden.at[:, block_cols(q, 1 - core)],
            dst_ref=held.at[q, pl.ds(tok, tok)],
            send_sem=hid_send.at[q],
            recv_sem=hid_recv.at[q],
            device_id=mate,
            device_id_type=MESH,
        )

    def send(name, src, dst, target):
        index = len(copies)
        copies[name] = pltpu.make_async_remote_copy(
            src_ref=src,
            dst_ref=dst,
            send_sem=send_sem.at[index],
            recv_sem=recv_sem.at[index],
            device_id=target,
            device_id_type=MESH,
        )
        copies[name].start()

    def arrived(name):
        copies[name].wait_recv()

    def loop_rows(count, body):
        @pl.loop(0, count // STEP)
        def _(i):
            body(pl.multiple_of(i * STEP, STEP))

    loads = [
        pltpu.make_async_copy(src, dst, raw_sem.at[i])
        for i, (src, dst) in enumerate(((weights, raw_weights), (anchor, raw_anchor), (key_grad, raw_grad), (tokens, raw_tokens)))
    ]
    for load in loads:
        load.start()

    @pl.loop(0, 16)
    def _(q):
        hidden_local(q).start()

    barrier = pltpu.get_barrier_semaphore()
    partners = (mate, across, up, down, beside, *along.values())
    for target in partners:
        pl.semaphore_signal(barrier, inc=1, device_id=target, device_id_type=MESH)
    own = slot(0, 0)
    loads[0].wait()

    def cast(r):
        wire[own, pl.ds(r, STEP)] = raw_weights[pl.ds(r, STEP)].astype(BF16)

    loop_rows(BLOCK, cast)
    pl.semaphore_wait(barrier, len(partners))

    send("ay0", wire.at[own, rows_a], wire.at[slot(0, 1), rows_a], across)
    for s in (1, -1):
        send(("az", s, 1, 0), wire.at[own], wire.at[slot(-s, 0)], toward[s])

    @pl.loop(0, 2)
    def _(q):
        hidden_remote(q).start()

    loads[2].wait()
    loads[3].wait()
    live = (raw_tokens[...] != 0).astype(F32)
    live_rows = jnp.transpose(jnp.broadcast_to(live, (128, tok))).astype(BF16)
    for j in range(width // 128):
        at = pl.ds(j * 128, 128)
        grads_in[pl.ds(0, tok), at] = raw_grad[:, at] * live_rows
    count_pair[...] = jnp.broadcast_to(jnp.sum(live, axis=1, keepdims=True), count_pair.shape)
    send("count_mate", count_pair, count_mate, mate)
    send("mask", grads_in.at[pl.ds(0, tok)], grads_in.at[pl.ds(tok, tok)], mate)

    @pl.loop(2, 16)
    def _(q):
        hidden_remote(q).start()

    loads[1].wait()
    in_second = fragment[0].astype(F32)

    def subtract(r):
        at = pl.ds(r, STEP)
        gap = raw_anchor[at] - raw_weights[at]
        differ[at] = gap[:, :half] * (1.0 - in_second) + gap[:, half:] * in_second

    loop_rows(BLOCK, subtract)

    for e in range(1, NX):
        at = pl.ds(pl.multiple_of(lax.rem(x + e, NX) * quarter, quarter), quarter)
        send(("dx", e), differ.at[at], from_x.at[e - 1], along[e])
    own_quarter = pl.ds(pl.multiple_of(x * quarter, quarter), quarter)

    def difference_x():
        for e in range(1, NX):
            arrived(("dx", e))
        piece[...] = differ[own_quarter] + from_x[0] + from_x[1] + from_x[2]
        send("dy", piece, from_y, beside)

    def difference_y():
        arrived("dy")
        delta[own_quarter] = (piece[...] + from_y[...]) * (1.0 / 8.0)
        for e in range(1, NX):
            send(("dg", e), delta.at[own_quarter], delta.at[own_quarter], along[e])

    def count_hop(k):
        if k == 1:
            arrived("count_mate")
            counts[0] = count_pair[...] + count_mate[...]
        for s in (1, -1):
            if k > 1:
                arrived(("cz", s, k - 1))
            if k < 4 or s == 1:
                send(("cz", s, k), counts.at[(-s * (k - 1)) % NZ], counts.at[(-s * k) % NZ], toward[s])

    def count_column():
        arrived(("cz", 1, 4))
        total = counts[0]
        for i in range(1, NZ):
            total = total + counts[i]
        count_total[...] = total
        send("count_across", count_total, count_across, across)

    def gather_hop(k, p):
        for s in (1, -1):
            src = slot(-s * (k - 1), p)
            dst = slot(4 if k == 4 else -s * k, p)
            rows = pl.ds(0, BLOCK) if p == 0 else rows_a
            if k > 1:
                arrived(("az", s, k - 1, p))
            if k == 4:
                send(("az", s, k, p), wire.at[src, rows, cols[s]], wire.at[dst, rows, cols[s]], toward[s])
            else:
                send(("az", s, k, p), wire.at[src, rows], wire.at[dst, rows], toward[s])
            if p == 0 and k > 1:
                send(("ayB", src), wire.at[src, rows_b], wire.at[src + 1, rows_b], across)

    def gather_step(k):
        count_hop(k)
        gather_hop(k, 0)
        gather_hop(k, 1)

    def gradient(*distances):
        first = order(distances[0])

        @pl.loop(2 * first, 2 * (first + len(distances)))
        def _(q):
            hidden_local(q).wait()
            hidden_remote(q).wait_recv()
            parts[q] = lax.dot_general(
                held[q], grads_in[...], (((0,), (0,)), ((), ())), preferred_element_type=F32
            )

        for d in distances:
            o = order(d)

            def stage(r, o=o):
                send_y[o, pl.ds(r, STEP)] = parts[2 * o + 1, pl.ds(ROWS_A + r, STEP)].astype(BF16)

            loop_rows(ROWS_B, stage)

    def part_y(*distances):
        for d in distances:
            send(("ry", d), send_y.at[order(d)], recv_y.at[order(d)], across)

    def reduce_far(p):
        for s in (1, -1):
            def stage(r, s=s):
                here = parts[slot(4, p), pl.ds(r, STEP), cols[s]]
                send_z[0 if s == 1 else 1, 3, pl.ds(p * BLOCK + r, STEP), cols[s]] = here.astype(BF16)

            def stage_b(r, s=s):
                here = parts[slot(4, p), pl.ds(ROWS_A + r, STEP), cols[s]]
                here = here + recv_y[order(4), pl.ds(r, STEP), cols[s]].astype(F32)
                send_z[0 if s == 1 else 1, 3, pl.ds(ROWS_A + r, STEP), cols[s]] = here.astype(BF16)

            loop_rows(ROWS_A, stage)
            if p == 0:
                if s == 1:
                    arrived(("ry", 4))
                loop_rows(ROWS_B, stage_b)
            rows = pl.ds(0, BLOCK) if p == 0 else pl.ds(BLOCK, ROWS_A)
            w = 0 if s == 1 else 1
            send(("rz", s, 4, p), send_z.at[w, 3, rows, cols[s]], recv_z.at[w, 3, rows, cols[s]], toward[s])

    def reduce_hop(d, p):
        for s in (1, -1):
            w = 0 if s == 1 else 1
            arrived(("rz", s, d + 1, p))
            if p == 0:
                arrived(("ry", s * d))

            def put(r, base, with_y, s=s, w=w):
                here = parts[slot(s * d, p), pl.ds(base + r, STEP)]
                at = pl.ds(p * BLOCK + base + r, STEP)
                if with_y:
                    here = here + recv_y[order(s * d), pl.ds(r, STEP)].astype(F32)
                if d == 3:
                    lo = 0 if s == 1 else half
                    there = recv_z[w, d, at, cols[s]].astype(F32)
                    summed = here[:, lo:lo + half] + there
                    send_z[w, d - 1, at, cols[s]] = summed.astype(BF16)
                    send_z[w, d - 1, at, cols[-s]] = here[:, half - lo:2 * half - lo].astype(BF16)
                else:
                    there = recv_z[w, d, at].astype(F32)
                    send_z[w, d - 1, at] = (here + there).astype(BF16)

            loop_rows(ROWS_A, lambda r: put(r, 0, False))
            if p == 0:
                loop_rows(ROWS_B, lambda r: put(r, ROWS_A, True))
            rows = pl.ds(0, BLOCK) if p == 0 else pl.ds(BLOCK, ROWS_A)
            send(("rz", s, d, p), send_z.at[w, d - 1, rows], recv_z.at[w, d - 1, rows], toward[s])

    def keys(*distances):
        for d in distances:
            q = slot(d, 0)
            if d == 0:
                arrived("ayB0")
            elif d == 4:
                arrived(("ayB", 4, 1))
                arrived(("ayB", 4, -1))
            else:
                arrived(("ayB", q))
            acc[...] += jnp.dot(held[q], wire[q], preferred_element_type=F32) + jnp.dot(
                held[q + 1], wire[q + 1], preferred_element_type=F32
            )

    arrived("mask")
    gradient(4)
    part_y(4)
    reduce_far(1)
    count_hop(1)
    arrived("ay0")
    gather_hop(1, 1)
    send("ayB0", wire.at[own, rows_b], wire.at[slot(0, 1), rows_b], across)
    gradient(3, -3)
    part_y(3, -3)
    count_hop(2)
    gather_hop(2, 0)
    reduce_far(0)
    gather_hop(2, 1)
    difference_x()
    gradient(2, -2)
    part_y(2, -2)
    reduce_hop(3, 1)
    reduce_hop(3, 0)
    gather_step(3)
    difference_y()
    gradient(1, -1, 0)
    part_y(1, -1)
    acc[...] = jnp.zeros_like(acc)
    reduce_hop(2, 1)
    gather_step(4)
    reduce_hop(2, 0)
    keys(0)
    reduce_hop(1, 1)
    count_column()
    for s in (1, -1):
        arrived(("az", s, 4, 0))
        src = slot(4, 0)
        send(("ayB", 4, s), wire.at[src, rows_b, cols[s]], wire.at[src + 1, rows_b, cols[s]], across)
    part_y(0)
    keys(1, -1)
    reduce_hop(1, 0)
    keys(2, -2, 3, -3)
    for e in range(1, NX):
        arrived(("dg", e))
    delta_out[...] = delta[...]

    for s in (1, -1):
        arrived(("rz", s, 1, 1))

    def close_a(r):
        at = pl.ds(BLOCK + r, STEP)
        total = parts[slot(0, 1), pl.ds(r, STEP)] + recv_z[0, 0, at].astype(F32) + recv_z[1, 0, at].astype(F32)
        send_a[pl.ds(r, STEP)] = total.astype(BF16)

    loop_rows(ROWS_A, close_a)
    send("rya", send_a, recv_a, across)
    for s in (1, -1):
        arrived(("az", s, 4, 1))
    arrived("count_across")
    scale = ((1.0 / math.sqrt(D)) / (count_total[...] + count_across[...]))[0:1, 0:1]
    keys(4)
    send("keys", acc.at[pl.ds(tok, tok)], other, mate)
    arrived("keys")

    def close_keys(r):
        at = pl.ds(r, STEP)
        keys_out[at] = ((acc[at] + other[at]) * (1.0 / math.sqrt(D))).astype(BF16)

    loop_rows(tok, close_keys)
    for s in (1, -1):
        arrived(("rz", s, 1, 0))
    arrived(("ry", 0))

    def close_b(r):
        at = pl.ds(ROWS_A + r, STEP)
        total = parts[slot(0, 0), at] + recv_y[order(0), pl.ds(r, STEP)].astype(F32)
        grad_out[at] = (total + recv_z[0, 0, at].astype(F32) + recv_z[1, 0, at].astype(F32)) * scale

    loop_rows(ROWS_B, close_b)
    arrived("rya")

    def close_all(r):
        at = pl.ds(r, STEP)
        total = parts[slot(0, 0), at] + recv_a[at].astype(F32)
        grad_out[at] = (total + recv_z[0, 0, at].astype(F32) + recv_z[1, 0, at].astype(F32)) * scale

    loop_rows(ROWS_A, close_all)
    for copy in copies.values():
        copy.wait_send()

    @pl.loop(0, 16)
    def _(q):
        hidden_remote(q).wait_send()


def exchange(hidden, tokens, key_grad, weights, anchor, fragment):
    tok, width = key_grad.shape
    half = width // 2
    vmem = pl.BlockSpec(memory_space=pltpu.VMEM)
    smem = pl.BlockSpec(memory_space=pltpu.SMEM)
    anywhere = pl.BlockSpec(memory_space=pl.ANY)
    hbm = pl.BlockSpec(memory_space=pltpu.HBM)
    count = 96
    tile = pltpu.VMEM((8, 128), F32)
    return pl.pallas_call(
        kernel,
        out_shape=(
            jax.ShapeDtypeStruct((BLOCK, width), F32),
            jax.ShapeDtypeStruct((tok, width), BF16),
            jax.ShapeDtypeStruct((BLOCK, half), F32),
        ),
        in_specs=[hbm] * 5 + [smem],
        out_specs=(vmem, vmem, vmem),
        scratch_shapes=[
            pltpu.VMEM((16, 2 * tok, BLOCK), BF16),
            pltpu.VMEM((2 * tok, width), BF16),
            pltpu.VMEM((16, BLOCK, width), F32),
            pltpu.VMEM((16, BLOCK, width), BF16),
            pltpu.VMEM((2 * tok, width), F32),
            pltpu.VMEM((tok, width), F32),
            pltpu.VMEM((2, 4, BLOCK + ROWS_A, width), BF16),
            pltpu.VMEM((2, 4, BLOCK + ROWS_A, width), BF16),
            pltpu.VMEM((8, ROWS_B, width), BF16),
            pltpu.VMEM((8, ROWS_B, width), BF16),
            pltpu.VMEM((ROWS_A, width), BF16),
            pltpu.VMEM((ROWS_A, width), BF16),
            pltpu.VMEM((tok, width), BF16),
            pltpu.VMEM((BLOCK, width), F32),
            pltpu.VMEM((BLOCK, width), F32),
            pltpu.VMEM(tokens.shape, jnp.int32),
            pltpu.VMEM((BLOCK, half), F32),
            pltpu.VMEM((NX - 1, BLOCK // NX, half), F32),
            pltpu.VMEM((BLOCK // NX, half), F32),
            pltpu.VMEM((BLOCK // NX, half), F32),
            pltpu.VMEM((BLOCK, half), F32),
            pltpu.VMEM((NZ, 8, 128), F32),
            tile,
            tile,
            tile,
            tile,
            pltpu.SemaphoreType.DMA((16,)),
            pltpu.SemaphoreType.DMA((4,)),
            pltpu.SemaphoreType.DMA((count,)),
            pltpu.SemaphoreType.DMA((count,)),
            pltpu.SemaphoreType.DMA((16,)),
            pltpu.SemaphoreType.DMA((16,)),
        ],
        compiler_params=pltpu.CompilerParams(
            collective_id=0, has_side_effects=True, vmem_limit_bytes=46 * 2**20
        ),
        cost_estimate=pl.CostEstimate(flops=13 * 10**9, bytes_accessed=16 * 2**20, transcendentals=0),
    )(hidden, tokens, key_grad, weights, anchor, fragment)


def finish_kernel(
    grad, delta, keys, first, second, weights, anchor, momentum, fragment, step_count,
    keys_out, weights_out, first_out, second_out, anchor_out, momentum_out,
    new_weights, new_first, new_second, new_anchor, new_momentum, sems,
):
    rows, width = grad.shape
    half = width // 2
    part = rows // FINISH_PARTS
    writes = [pltpu.make_async_copy(keys, keys_out, sems.at[0])]
    writes[0].start()

    def write(src, dst, at):
        writes.append(pltpu.make_async_copy(src.at[at], dst.at[at], sems.at[len(writes)]))
        writes[-1].start()

    steps = jnp.full((1, half), step_count[0], jnp.int32).astype(F32)
    first_scale = 1.0 / (1.0 - jnp.exp(steps * math.log(BETA_ONE)))
    second_scale = 1.0 / (1.0 - jnp.exp(steps * math.log(BETA_TWO)))
    for i in range(FINISH_PARTS):
        at = pl.ds(i * part, part)
        gap = delta[at]
        for h in range(FRAGS):
            cols = pl.ds(h * half, half)
            moved = fragment[0] == h
            old_anchor, old_momentum = anchor[at, cols], momentum[at, cols]
            moved_momentum = OUTER_MOMENTUM * old_momentum + gap
            moved_anchor = old_anchor - OUTER_LR * (gap + OUTER_MOMENTUM * moved_momentum)
            new_momentum[at, cols] = jnp.where(moved, moved_momentum, old_momentum)
            new_anchor[at, cols] = jnp.where(moved, moved_anchor, old_anchor)
            gradient = grad[at, cols]
            one = BETA_ONE * first[at, cols] + (1.0 - BETA_ONE) * gradient
            two = BETA_TWO * second[at, cols] + (1.0 - BETA_TWO) * gradient * gradient
            new_first[at, cols] = one
            new_second[at, cols] = two
            ratio = one * first_scale / (jnp.sqrt(two * second_scale) + EPSILON)
            old = weights[at, cols]
            stepped = old - INNER_LR * (ratio + WEIGHT_DECAY * old)
            mixed = MIX_LOCAL * stepped + (1.0 - MIX_LOCAL) * moved_anchor
            new_weights[at, cols] = jnp.where(moved, mixed, stepped)
        write(new_momentum, momentum_out, at)
        write(new_anchor, anchor_out, at)
        write(new_first, first_out, at)
        write(new_second, second_out, at)
        write(new_weights, weights_out, at)
    for copy in writes:
        copy.wait()


FINISH_PARTS = 4


def finish(grad, delta, keys, first, second, weights, anchor, momentum, fragment, step_count):
    vmem = pl.BlockSpec(memory_space=pltpu.VMEM)
    smem = pl.BlockSpec(memory_space=pltpu.SMEM)
    anywhere = pl.BlockSpec(memory_space=pl.ANY)
    block = jax.ShapeDtypeStruct(grad.shape, F32)
    return pl.pallas_call(
        finish_kernel,
        out_shape=(jax.ShapeDtypeStruct(keys.shape, keys.dtype),) + (block,) * 5,
        in_specs=[vmem, vmem, anywhere] + [vmem] * 5 + [smem, smem],
        out_specs=(anywhere,) * 6,
        scratch_shapes=[pltpu.VMEM(grad.shape, F32)] * 5 + [pltpu.SemaphoreType.DMA((1 + 5 * FINISH_PARTS,))],
        compiler_params=pltpu.CompilerParams(vmem_limit_bytes=16 * 2**20),
    )(grad, delta, keys, first, second, weights, anchor, momentum, fragment, step_count)


def on_device(
    hidden,
    token_ids,
    key_grad,
    weights,
    first_moment,
    second_moment,
    anchor,
    momentum,
    fragment,
    step_count,
):
    operands = [
        pltpu.with_memory_space_constraint(operand, pltpu.HBM)
        for operand in (hidden[0], token_ids, key_grad[0], weights[0], anchor)
    ]
    grad, keys, delta = exchange(*operands, fragment)
    keys, new_weights, new_first, new_second, new_anchor, new_momentum = finish(
        grad, delta, keys, first_moment[0], second_moment[0], weights[0], anchor, momentum, fragment, step_count
    )
    return keys[None], new_weights[None], new_first[None], new_second[None], new_anchor, new_momentum


def solution(mesh):
    return jax.shard_map(
        on_device,
        mesh=mesh,
        in_specs=(
            P("rep", "fsdp", None),
            P("rep", "fsdp"),
            P("rep", "fsdp", None),
            P("rep", "fsdp", None),
            P("rep", "fsdp", None),
            P("rep", "fsdp", None),
            P("fsdp", None),
            P("fsdp", None),
            P(),
            P(),
        ),
        out_specs=(
            P("rep", "fsdp", None),
            P("rep", "fsdp", None),
            P("rep", "fsdp", None),
            P("rep", "fsdp", None),
            P("fsdp", None),
            P("fsdp", None),
        ),
        check_vma=False,
    )
```

```python
import math

import jax
import jax.numpy as jnp
from jax import lax
from jax.experimental import pallas as pl
from jax.experimental.pallas import tpu as pltpu
from jax.sharding import PartitionSpec as P

MESH = pl.DeviceIdType.MESH
BF16, F32 = jnp.bfloat16, jnp.float32

D = 8192
FRAGS = 2
NZ = 8
NX = 4
BLOCK = 256
ROWS_G = 144
ROWS_A = 80
ROWS_B = BLOCK - ROWS_A
STEP = 16

BETA_ONE = 0.9
BETA_TWO = 0.95
EPSILON = 1e-08
INNER_LR = 0.1
WEIGHT_DECAY = 0.1
OUTER_LR = 0.7
OUTER_MOMENTUM = 0.9
MIX_LOCAL = 0.5


def order(d):
    return {4: 0, 3: 1, -3: 2, 2: 3, -2: 4, 1: 5, -1: 6, 0: 7}[d]


def slot(d, p):
    return 2 * order(d) + p


def distance(o):
    far = 4 - (o + 1) // 2
    return jnp.where(o % 2 == 1, far, -far)


def kernel(
    hidden, tokens, key_grad, weights, anchor, fragment, grad_out, keys_out, delta_out,
    held, grads_in, parts, wire, acc, other, send_z, recv_z, send_y, recv_y, send_a, recv_a,
    raw_grad, raw_weights, raw_anchor, raw_tokens, differ, from_x, piece, from_y, delta, counts, count_mate, count_pair, count_across, count_total,
    local_sem, raw_sem, send_sem, recv_sem, hid_send, hid_recv,
):
    tok, width = key_grad.shape
    half = width // 2
    quarter = BLOCK // NX
    rep = lax.axis_index("rep")
    me = lax.axis_index("fsdp")
    z, yh, core = me // 4, (me // 2) % 2, me % 2
    yl, x = rep // NX, rep % NX
    mate = (rep, z * 4 + yh * 2 + (1 - core))
    across = (rep, z * 4 + (1 - yh) * 2 + core)
    up = (rep, lax.rem(z + 1, NZ) * 4 + yh * 2 + core)
    down = (rep, lax.rem(z + NZ - 1, NZ) * 4 + yh * 2 + core)
    toward = {1: up, -1: down}
    beside = ((1 - yl) * NX + x, me)
    along = {e: (yl * NX + lax.rem(x + e, NX), me) for e in range(1, NX)}
    rows_a, rows_b = pl.ds(0, ROWS_G), pl.ds(ROWS_G, BLOCK - ROWS_G)
    cols = {1: pl.ds(0, half), -1: pl.ds(half, half)}
    copies = {}

    def block_cols(q, c):
        d, p = distance(q // 2), q % 2
        zz = lax.rem(z + d + 2 * NZ, NZ)
        yy = lax.rem(yh + p, 2)
        return pl.ds(pl.multiple_of((zz * 4 + yy * 2 + c) * BLOCK, BLOCK), BLOCK)

    def hidden_local(q):
        return pltpu.make_async_copy(
            hidden.at[:, block_cols(q, core)], held.at[q, pl.ds(0, tok)], local_sem.at[q]
        )

    def hidden_remote(q):
        return pltpu.make_async_remote_copy(
            src_ref=hidden.at[:, block_cols(q, 1 - core)],
            dst_ref=held.at[q, pl.ds(tok, tok)],
            send_sem=hid_send.at[q],
            recv_sem=hid_recv.at[q],
            device_id=mate,
            device_id_type=MESH,
        )

    def send(name, src, dst, target):
        index = len(copies)
        copies[name] = pltpu.make_async_remote_copy(
            src_ref=src,
            dst_ref=dst,
            send_sem=send_sem.at[index],
            recv_sem=recv_sem.at[index],
            device_id=target,
            device_id_type=MESH,
        )
        copies[name].start()

    def arrived(name):
        copies[name].wait_recv()

    def loop_rows(count, body):
        @pl.loop(0, count // STEP)
        def _(i):
            body(pl.multiple_of(i * STEP, STEP))

    barrier = pltpu.get_barrier_semaphore()
    partners = (mate, across, up, down, beside, *along.values())
    for target in partners:
        pl.semaphore_signal(barrier, inc=1, device_id=target, device_id_type=MESH)
    loads = [
        pltpu.make_async_copy(src, dst, raw_sem.at[i])
        for i, (src, dst) in enumerate(((weights, raw_weights), (anchor, raw_anchor), (key_grad, raw_grad), (tokens, raw_tokens)))
    ]
    for load in loads:
        load.start()

    own = slot(0, 0)
    loads[0].wait()

    def cast(r):
        wire[own, pl.ds(r, STEP)] = raw_weights[pl.ds(r, STEP)].astype(BF16)

    loop_rows(BLOCK, cast)
    pl.semaphore_wait(barrier, len(partners))

    send("ay0", wire.at[own, rows_a], wire.at[slot(0, 1), rows_a], across)
    for s in (1, -1):
        send(("az", s, 1, 0), wire.at[own], wire.at[slot(-s, 0)], toward[s])

    @pl.loop(0, 16)
    def _(q):
        hidden_local(q).start()

    @pl.loop(0, 2)
    def _(q):
        hidden_remote(q).start()

    loads[2].wait()
    loads[3].wait()
    live = (raw_tokens[...] != 0).astype(F32)
    live_rows = jnp.transpose(jnp.broadcast_to(live, (128, tok))).astype(BF16)
    for j in range(width // 128):
        at = pl.ds(j * 128, 128)
        grads_in[pl.ds(0, tok), at] = raw_grad[:, at] * live_rows
    count_pair[...] = jnp.broadcast_to(jnp.sum(live, axis=1, keepdims=True), count_pair.shape)
    send("count_mate", count_pair, count_mate, mate)
    send("mask", grads_in.at[pl.ds(0, tok)], grads_in.at[pl.ds(tok, tok)], mate)

    @pl.loop(2, 16)
    def _(q):
        hidden_remote(q).start()

    loads[1].wait()
    in_second = fragment[0].astype(F32)

    def subtract(r):
        at = pl.ds(r, STEP)
        gap = raw_anchor[at] - raw_weights[at]
        differ[at] = gap[:, :half] * (1.0 - in_second) + gap[:, half:] * in_second

    loop_rows(BLOCK, subtract)

    for e in range(1, NX):
        at = pl.ds(pl.multiple_of(lax.rem(x + e, NX) * quarter, quarter), quarter)
        send(("dx", e), differ.at[at], from_x.at[e - 1], along[e])
    own_quarter = pl.ds(pl.multiple_of(x * quarter, quarter), quarter)

    def difference_x():
        for e in range(1, NX):
            arrived(("dx", e))
        piece[...] = differ[own_quarter] + from_x[0] + from_x[1] + from_x[2]
        send("dy", piece, from_y, beside)

    def difference_y():
        arrived("dy")
        delta[own_quarter] = (piece[...] + from_y[...]) * (1.0 / 8.0)
        for e in range(1, NX):
            send(("dg", e), delta.at[own_quarter], delta.at[own_quarter], along[e])

    def count_hop(k):
        if k == 1:
            arrived("count_mate")
            counts[0] = count_pair[...] + count_mate[...]
        for s in (1, -1):
            if k > 1:
                arrived(("cz", s, k - 1))
            if k < 4 or s == 1:
                send(("cz", s, k), counts.at[(-s * (k - 1)) % NZ], counts.at[(-s * k) % NZ], toward[s])

    def count_column():
        arrived(("cz", 1, 4))
        total = counts[0]
        for i in range(1, NZ):
            total = total + counts[i]
        count_total[...] = total
        send("count_across", count_total, count_across, across)

    def gather_hop(k, p):
        for s in (1, -1):
            src = slot(-s * (k - 1), p)
            dst = slot(4 if k == 4 else -s * k, p)
            rows = pl.ds(0, BLOCK) if p == 0 else rows_a
            if k > 1:
                arrived(("az", s, k - 1, p))
            if k == 4:
                send(("az", s, k, p), wire.at[src, rows, cols[s]], wire.at[dst, rows, cols[s]], toward[s])
            else:
                send(("az", s, k, p), wire.at[src, rows], wire.at[dst, rows], toward[s])
            if p == 0 and k > 1:
                send(("ayB", src), wire.at[src, rows_b], wire.at[src + 1, rows_b], across)

    def gather_step(k):
        count_hop(k)
        gather_hop(k, 0)
        gather_hop(k, 1)

    def gradient(*distances):
        first = order(distances[0])

        @pl.loop(2 * first, 2 * (first + len(distances)))
        def _(q):
            hidden_local(q).wait()
            hidden_remote(q).wait_recv()
            parts[q] = lax.dot_general(
                held[q], grads_in[...], (((0,), (0,)), ((), ())), preferred_element_type=F32
            )

        for d in distances:
            o = order(d)

            def stage(r, o=o):
                send_y[o, pl.ds(r, STEP)] = parts[2 * o + 1, pl.ds(ROWS_A + r, STEP)].astype(BF16)

            loop_rows(ROWS_B, stage)

    def part_y(*distances):
        for d in distances:
            send(("ry", d), send_y.at[order(d)], recv_y.at[order(d)], across)

    def reduce_far(p):
        for s in (1, -1):
            def stage(r, s=s):
                here = parts[slot(4, p), pl.ds(r, STEP), cols[s]]
                send_z[0 if s == 1 else 1, 3, pl.ds(p * BLOCK + r, STEP), cols[s]] = here.astype(BF16)

            def stage_b(r, s=s):
                here = parts[slot(4, p), pl.ds(ROWS_A + r, STEP), cols[s]]
                here = here + recv_y[order(4), pl.ds(r, STEP), cols[s]].astype(F32)
                send_z[0 if s == 1 else 1, 3, pl.ds(ROWS_A + r, STEP), cols[s]] = here.astype(BF16)

            loop_rows(ROWS_A, stage)
            if p == 0:
                if s == 1:
                    arrived(("ry", 4))
                loop_rows(ROWS_B, stage_b)
            rows = pl.ds(0, BLOCK) if p == 0 else pl.ds(BLOCK, ROWS_A)
            w = 0 if s == 1 else 1
            send(("rz", s, 4, p), send_z.at[w, 3, rows, cols[s]], recv_z.at[w, 3, rows, cols[s]], toward[s])

    def reduce_hop(d, p):
        for s in (1, -1):
            w = 0 if s == 1 else 1
            arrived(("rz", s, d + 1, p))
            if p == 0:
                arrived(("ry", s * d))

            def put(r, base, with_y, s=s, w=w):
                here = parts[slot(s * d, p), pl.ds(base + r, STEP)]
                at = pl.ds(p * BLOCK + base + r, STEP)
                if with_y:
                    here = here + recv_y[order(s * d), pl.ds(r, STEP)].astype(F32)
                if d == 3:
                    lo = 0 if s == 1 else half
                    there = recv_z[w, d, at, cols[s]].astype(F32)
                    summed = here[:, lo:lo + half] + there
                    send_z[w, d - 1, at, cols[s]] = summed.astype(BF16)
                    send_z[w, d - 1, at, cols[-s]] = here[:, half - lo:2 * half - lo].astype(BF16)
                else:
                    there = recv_z[w, d, at].astype(F32)
                    send_z[w, d - 1, at] = (here + there).astype(BF16)

            loop_rows(ROWS_A, lambda r: put(r, 0, False))
            if p == 0:
                loop_rows(ROWS_B, lambda r: put(r, ROWS_A, True))
            rows = pl.ds(0, BLOCK) if p == 0 else pl.ds(BLOCK, ROWS_A)
            send(("rz", s, d, p), send_z.at[w, d - 1, rows], recv_z.at[w, d - 1, rows], toward[s])

    def keys(*distances):
        for d in distances:
            q = slot(d, 0)
            if d == 0:
                arrived("ayB0")
            elif d == 4:
                arrived(("ayB", 4, 1))
                arrived(("ayB", 4, -1))
            else:
                arrived(("ayB", q))
            acc[...] += jnp.dot(held[q], wire[q], preferred_element_type=F32) + jnp.dot(
                held[q + 1], wire[q + 1], preferred_element_type=F32
            )

    arrived("mask")
    gradient(4)
    part_y(4)
    reduce_far(1)
    count_hop(1)
    arrived("ay0")
    gather_hop(1, 1)
    send("ayB0", wire.at[own, rows_b], wire.at[slot(0, 1), rows_b], across)
    gradient(3, -3)
    part_y(3, -3)
    count_hop(2)
    gather_hop(2, 0)
    reduce_far(0)
    gather_hop(2, 1)
    difference_x()
    gradient(2, -2)
    part_y(2, -2)
    reduce_hop(3, 1)
    reduce_hop(3, 0)
    gather_step(3)
    difference_y()
    gradient(1, -1, 0)
    part_y(1, -1)
    acc[...] = jnp.zeros_like(acc)
    reduce_hop(2, 1)
    gather_step(4)
    reduce_hop(2, 0)
    keys(0)
    reduce_hop(1, 1)
    count_column()
    for s in (1, -1):
        arrived(("az", s, 4, 0))
        src = slot(4, 0)
        send(("ayB", 4, s), wire.at[src, rows_b, cols[s]], wire.at[src + 1, rows_b, cols[s]], across)
    part_y(0)
    keys(1, -1)
    reduce_hop(1, 0)
    keys(2, -2, 3, -3)
    for e in range(1, NX):
        arrived(("dg", e))
    delta_out[...] = delta[...]

    for s in (1, -1):
        arrived(("rz", s, 1, 1))

    def close_a(r):
        at = pl.ds(BLOCK + r, STEP)
        total = parts[slot(0, 1), pl.ds(r, STEP)] + recv_z[0, 0, at].astype(F32) + recv_z[1, 0, at].astype(F32)
        send_a[pl.ds(r, STEP)] = total.astype(BF16)

    loop_rows(ROWS_A, close_a)
    send("rya", send_a, recv_a, across)
    for s in (1, -1):
        arrived(("az", s, 4, 1))
    arrived("count_across")
    scale = ((1.0 / math.sqrt(D)) / (count_total[...] + count_across[...]))[0:1, 0:1]
    keys(4)
    send("keys", acc.at[pl.ds(tok, tok)], other, mate)
    arrived("keys")

    def close_keys(r):
        at = pl.ds(r, STEP)
        keys_out[at] = ((acc[at] + other[at]) * (1.0 / math.sqrt(D))).astype(BF16)

    loop_rows(tok, close_keys)
    for s in (1, -1):
        arrived(("rz", s, 1, 0))
    arrived(("ry", 0))

    def close_b(r):
        at = pl.ds(ROWS_A + r, STEP)
        total = parts[slot(0, 0), at] + recv_y[order(0), pl.ds(r, STEP)].astype(F32)
        grad_out[at] = (total + recv_z[0, 0, at].astype(F32) + recv_z[1, 0, at].astype(F32)) * scale

    loop_rows(ROWS_B, close_b)
    arrived("rya")

    def close_all(r):
        at = pl.ds(r, STEP)
        total = parts[slot(0, 0), at] + recv_a[at].astype(F32)
        grad_out[at] = (total + recv_z[0, 0, at].astype(F32) + recv_z[1, 0, at].astype(F32)) * scale

    loop_rows(ROWS_A, close_all)
    for copy in copies.values():
        copy.wait_send()

    @pl.loop(0, 16)
    def _(q):
        hidden_remote(q).wait_send()


def exchange(hidden, tokens, key_grad, weights, anchor, fragment):
    tok, width = key_grad.shape
    half = width // 2
    vmem = pl.BlockSpec(memory_space=pltpu.VMEM)
    smem = pl.BlockSpec(memory_space=pltpu.SMEM)
    anywhere = pl.BlockSpec(memory_space=pl.ANY)
    hbm = pl.BlockSpec(memory_space=pltpu.HBM)
    count = 96
    tile = pltpu.VMEM((8, 128), F32)
    return pl.pallas_call(
        kernel,
        out_shape=(
            jax.ShapeDtypeStruct((BLOCK, width), F32),
            jax.ShapeDtypeStruct((tok, width), BF16),
            jax.ShapeDtypeStruct((BLOCK, half), F32),
        ),
        in_specs=[hbm] * 5 + [smem],
        out_specs=(vmem, vmem, vmem),
        scratch_shapes=[
            pltpu.VMEM((16, 2 * tok, BLOCK), BF16),
            pltpu.VMEM((2 * tok, width), BF16),
            pltpu.VMEM((16, BLOCK, width), F32),
            pltpu.VMEM((16, BLOCK, width), BF16),
            pltpu.VMEM((2 * tok, width), F32),
            pltpu.VMEM((tok, width), F32),
            pltpu.VMEM((2, 4, BLOCK + ROWS_A, width), BF16),
            pltpu.VMEM((2, 4, BLOCK + ROWS_A, width), BF16),
            pltpu.VMEM((8, ROWS_B, width), BF16),
            pltpu.VMEM((8, ROWS_B, width), BF16),
            pltpu.VMEM((ROWS_A, width), BF16),
            pltpu.VMEM((ROWS_A, width), BF16),
            pltpu.VMEM((tok, width), BF16),
            pltpu.VMEM((BLOCK, width), F32),
            pltpu.VMEM((BLOCK, width), F32),
            pltpu.VMEM(tokens.shape, jnp.int32),
            pltpu.VMEM((BLOCK, half), F32),
            pltpu.VMEM((NX - 1, BLOCK // NX, half), F32),
            pltpu.VMEM((BLOCK // NX, half), F32),
            pltpu.VMEM((BLOCK // NX, half), F32),
            pltpu.VMEM((BLOCK, half), F32),
            pltpu.VMEM((NZ, 8, 128), F32),
            tile,
            tile,
            tile,
            tile,
            pltpu.SemaphoreType.DMA((16,)),
            pltpu.SemaphoreType.DMA((4,)),
            pltpu.SemaphoreType.DMA((count,)),
            pltpu.SemaphoreType.DMA((count,)),
            pltpu.SemaphoreType.DMA((16,)),
            pltpu.SemaphoreType.DMA((16,)),
        ],
        compiler_params=pltpu.CompilerParams(
            collective_id=0, has_side_effects=True, vmem_limit_bytes=46 * 2**20
        ),
        cost_estimate=pl.CostEstimate(flops=13 * 10**9, bytes_accessed=16 * 2**20, transcendentals=0),
    )(hidden, tokens, key_grad, weights, anchor, fragment)


def finish_kernel(
    grad, delta, keys, first, second, weights, anchor, momentum, fragment, step_count,
    keys_out, weights_out, first_out, second_out, anchor_out, momentum_out,
    new_weights, new_first, new_second, new_anchor, new_momentum, sems,
):
    rows, width = grad.shape
    half = width // 2
    part = rows // FINISH_PARTS
    writes = [pltpu.make_async_copy(keys, keys_out, sems.at[0])]
    writes[0].start()

    def write(src, dst, at):
        writes.append(pltpu.make_async_copy(src.at[at], dst.at[at], sems.at[len(writes)]))
        writes[-1].start()

    steps = jnp.full((1, half), step_count[0], jnp.int32).astype(F32)
    first_scale = 1.0 / (1.0 - jnp.exp(steps * math.log(BETA_ONE)))
    second_scale = 1.0 / (1.0 - jnp.exp(steps * math.log(BETA_TWO)))
    for i in range(FINISH_PARTS):
        at = pl.ds(i * part, part)
        gap = delta[at]
        for h in range(FRAGS):
            cols = pl.ds(h * half, half)
            moved = fragment[0] == h
            old_anchor, old_momentum = anchor[at, cols], momentum[at, cols]
            moved_momentum = OUTER_MOMENTUM * old_momentum + gap
            moved_anchor = old_anchor - OUTER_LR * (gap + OUTER_MOMENTUM * moved_momentum)
            new_momentum[at, cols] = jnp.where(moved, moved_momentum, old_momentum)
            new_anchor[at, cols] = jnp.where(moved, moved_anchor, old_anchor)
            gradient = grad[at, cols]
            one = BETA_ONE * first[at, cols] + (1.0 - BETA_ONE) * gradient
            two = BETA_TWO * second[at, cols] + (1.0 - BETA_TWO) * gradient * gradient
            new_first[at, cols] = one
            new_second[at, cols] = two
            ratio = one * first_scale / (jnp.sqrt(two * second_scale) + EPSILON)
            old = weights[at, cols]
            stepped = old - INNER_LR * (ratio + WEIGHT_DECAY * old)
            mixed = MIX_LOCAL * stepped + (1.0 - MIX_LOCAL) * moved_anchor
            new_weights[at, cols] = jnp.where(moved, mixed, stepped)
        write(new_momentum, momentum_out, at)
        write(new_anchor, anchor_out, at)
        write(new_first, first_out, at)
        write(new_second, second_out, at)
        write(new_weights, weights_out, at)
    for copy in writes:
        copy.wait()


FINISH_PARTS = 4


def finish(grad, delta, keys, first, second, weights, anchor, momentum, fragment, step_count):
    vmem = pl.BlockSpec(memory_space=pltpu.VMEM)
    smem = pl.BlockSpec(memory_space=pltpu.SMEM)
    anywhere = pl.BlockSpec(memory_space=pl.ANY)
    block = jax.ShapeDtypeStruct(grad.shape, F32)
    return pl.pallas_call(
        finish_kernel,
        out_shape=(jax.ShapeDtypeStruct(keys.shape, keys.dtype),) + (block,) * 5,
        in_specs=[vmem, vmem, anywhere] + [vmem] * 5 + [smem, smem],
        out_specs=(anywhere,) * 6,
        scratch_shapes=[pltpu.VMEM(grad.shape, F32)] * 5 + [pltpu.SemaphoreType.DMA((1 + 5 * FINISH_PARTS,))],
        compiler_params=pltpu.CompilerParams(vmem_limit_bytes=16 * 2**20),
    )(grad, delta, keys, first, second, weights, anchor, momentum, fragment, step_count)


def on_device(
    hidden,
    token_ids,
    key_grad,
    weights,
    first_moment,
    second_moment,
    anchor,
    momentum,
    fragment,
    step_count,
):
    operands = [
        pltpu.with_memory_space_constraint(operand, pltpu.HBM)
        for operand in (hidden[0], token_ids, key_grad[0], weights[0], anchor)
    ]
    grad, keys, delta = exchange(*operands, fragment)
    keys, new_weights, new_first, new_second, new_anchor, new_momentum = finish(
        grad, delta, keys, first_moment[0], second_moment[0], weights[0], anchor, momentum, fragment, step_count
    )
    return keys[None], new_weights[None], new_first[None], new_second[None], new_anchor, new_momentum


def solution(mesh):
    return jax.shard_map(
        on_device,
        mesh=mesh,
        in_specs=(
            P("rep", "fsdp", None),
            P("rep", "fsdp"),
            P("rep", "fsdp", None),
            P("rep", "fsdp", None),
            P("rep", "fsdp", None),
            P("rep", "fsdp", None),
            P("fsdp", None),
            P("fsdp", None),
            P(),
            P(),
        ),
        out_specs=(
            P("rep", "fsdp", None),
            P("rep", "fsdp", None),
            P("rep", "fsdp", None),
            P("rep", "fsdp", None),
            P("fsdp", None),
            P("fsdp", None),
        ),
        check_vma=False,
    )
```

```python
import math

import jax
import jax.numpy as jnp
from jax import lax
from jax.experimental import pallas as pl
from jax.experimental.pallas import tpu as pltpu
from jax.sharding import PartitionSpec as P

MESH = pl.DeviceIdType.MESH
BF16, F32 = jnp.bfloat16, jnp.float32

D = 8192
FRAGS = 2
NZ = 8
NX = 4
BLOCK = 256
ROWS_G = 160
ROWS_A = 64
ROWS_B = BLOCK - ROWS_A
STEP = 16

BETA_ONE = 0.9
BETA_TWO = 0.95
EPSILON = 1e-08
INNER_LR = 0.1
WEIGHT_DECAY = 0.1
OUTER_LR = 0.7
OUTER_MOMENTUM = 0.9
MIX_LOCAL = 0.5


def order(d):
    return {4: 0, 3: 1, -3: 2, 2: 3, -2: 4, 1: 5, -1: 6, 0: 7}[d]


def slot(d, p):
    return 2 * order(d) + p


def distance(o):
    far = 4 - (o + 1) // 2
    return jnp.where(o % 2 == 1, far, -far)


def kernel(
    hidden, tokens, key_grad, weights, anchor, fragment, grad_out, keys_out, delta_out,
    held, grads_in, parts, wire, acc, other, send_z, recv_z, send_y, recv_y, send_a, recv_a,
    raw_grad, raw_weights, raw_anchor, raw_tokens, differ, from_x, piece, from_y, delta, counts, count_mate, count_pair, count_across, count_total,
    local_sem, raw_sem, send_sem, recv_sem, hid_send, hid_recv,
):
    tok, width = key_grad.shape
    half = width // 2
    quarter = BLOCK // NX
    rep = lax.axis_index("rep")
    me = lax.axis_index("fsdp")
    z, yh, core = me // 4, (me // 2) % 2, me % 2
    yl, x = rep // NX, rep % NX
    mate = (rep, z * 4 + yh * 2 + (1 - core))
    across = (rep, z * 4 + (1 - yh) * 2 + core)
    up = (rep, lax.rem(z + 1, NZ) * 4 + yh * 2 + core)
    down = (rep, lax.rem(z + NZ - 1, NZ) * 4 + yh * 2 + core)
    toward = {1: up, -1: down}
    beside = ((1 - yl) * NX + x, me)
    along = {e: (yl * NX + lax.rem(x + e, NX), me) for e in range(1, NX)}
    rows_a, rows_b = pl.ds(0, ROWS_G), pl.ds(ROWS_G, BLOCK - ROWS_G)
    cols = {1: pl.ds(0, half), -1: pl.ds(half, half)}
    copies = {}

    def block_cols(q, c):
        d, p = distance(q // 2), q % 2
        zz = lax.rem(z + d + 2 * NZ, NZ)
        yy = lax.rem(yh + p, 2)
        return pl.ds(pl.multiple_of((zz * 4 + yy * 2 + c) * BLOCK, BLOCK), BLOCK)

    def hidden_local(q):
        return pltpu.make_async_copy(
            hidden.at[:, block_cols(q, core)], held.at[q, pl.ds(0, tok)], local_sem.at[q]
        )

    def hidden_remote(q):
        return pltpu.make_async_remote_copy(
            src_ref=hidden.at[:, block_cols(q, 1 - core)],
            dst_ref=held.at[q, pl.ds(tok, tok)],
            send_sem=hid_send.at[q],
            recv_sem=hid_recv.at[q],
            device_id=mate,
            device_id_type=MESH,
        )

    def send(name, src, dst, target):
        index = len(copies)
        copies[name] = pltpu.make_async_remote_copy(
            src_ref=src,
            dst_ref=dst,
            send_sem=send_sem.at[index],
            recv_sem=recv_sem.at[index],
            device_id=target,
            device_id_type=MESH,
        )
        copies[name].start()

    def arrived(name):
        copies[name].wait_recv()

    def loop_rows(count, body):
        @pl.loop(0, count // STEP)
        def _(i):
            body(pl.multiple_of(i * STEP, STEP))

    barrier = pltpu.get_barrier_semaphore()
    partners = (mate, across, up, down, beside, *along.values())
    for target in partners:
        pl.semaphore_signal(barrier, inc=1, device_id=target, device_id_type=MESH)
    loads = [
        pltpu.make_async_copy(src, dst, raw_sem.at[i])
        for i, (src, dst) in enumerate(((weights, raw_weights), (anchor, raw_anchor), (key_grad, raw_grad), (tokens, raw_tokens)))
    ]
    for load in loads:
        load.start()

    own = slot(0, 0)
    loads[0].wait()

    def cast(r):
        wire[own, pl.ds(r, STEP)] = raw_weights[pl.ds(r, STEP)].astype(BF16)

    loop_rows(BLOCK, cast)
    pl.semaphore_wait(barrier, len(partners))

    send("ay0", wire.at[own, rows_a], wire.at[slot(0, 1), rows_a], across)
    for s in (1, -1):
        send(("az", s, 1, 0), wire.at[own], wire.at[slot(-s, 0)], toward[s])

    @pl.loop(0, 16)
    def _(q):
        hidden_local(q).start()

    @pl.loop(0, 2)
    def _(q):
        hidden_remote(q).start()

    loads[2].wait()
    loads[3].wait()
    live = (raw_tokens[...] != 0).astype(F32)
    live_rows = jnp.transpose(jnp.broadcast_to(live, (128, tok))).astype(BF16)
    for j in range(width // 128):
        at = pl.ds(j * 128, 128)
        grads_in[pl.ds(0, tok), at] = raw_grad[:, at] * live_rows
    count_pair[...] = jnp.broadcast_to(jnp.sum(live, axis=1, keepdims=True), count_pair.shape)
    send("count_mate", count_pair, count_mate, mate)
    send("mask", grads_in.at[pl.ds(0, tok)], grads_in.at[pl.ds(tok, tok)], mate)

    @pl.loop(2, 16)
    def _(q):
        hidden_remote(q).start()

    loads[1].wait()
    in_second = fragment[0].astype(F32)

    def subtract(r):
        at = pl.ds(r, STEP)
        gap = raw_anchor[at] - raw_weights[at]
        differ[at] = gap[:, :half] * (1.0 - in_second) + gap[:, half:] * in_second

    loop_rows(BLOCK, subtract)

    for e in range(1, NX):
        at = pl.ds(pl.multiple_of(lax.rem(x + e, NX) * quarter, quarter), quarter)
        send(("dx", e), differ.at[at], from_x.at[e - 1], along[e])
    own_quarter = pl.ds(pl.multiple_of(x * quarter, quarter), quarter)

    def difference_x():
        for e in range(1, NX):
            arrived(("dx", e))
        piece[...] = differ[own_quarter] + from_x[0] + from_x[1] + from_x[2]
        send("dy", piece, from_y, beside)

    def difference_y():
        arrived("dy")
        delta[own_quarter] = (piece[...] + from_y[...]) * (1.0 / 8.0)
        for e in range(1, NX):
            send(("dg", e), delta.at[own_quarter], delta.at[own_quarter], along[e])

    def count_hop(k):
        if k == 1:
            arrived("count_mate")
            counts[0] = count_pair[...] + count_mate[...]
        for s in (1, -1):
            if k > 1:
                arrived(("cz", s, k - 1))
            if k < 4 or s == 1:
                send(("cz", s, k), counts.at[(-s * (k - 1)) % NZ], counts.at[(-s * k) % NZ], toward[s])

    def count_column():
        arrived(("cz", 1, 4))
        total = counts[0]
        for i in range(1, NZ):
            total = total + counts[i]
        count_total[...] = total
        send("count_across", count_total, count_across, across)

    def gather_hop(k, p):
        for s in (1, -1):
            src = slot(-s * (k - 1), p)
            dst = slot(4 if k == 4 else -s * k, p)
            rows = pl.ds(0, BLOCK) if p == 0 else rows_a
            if k > 1:
                arrived(("az", s, k - 1, p))
            if k == 4:
                send(("az", s, k, p), wire.at[src, rows, cols[s]], wire.at[dst, rows, cols[s]], toward[s])
            else:
                send(("az", s, k, p), wire.at[src, rows], wire.at[dst, rows], toward[s])
            if p == 0 and k > 1:
                send(("ayB", src), wire.at[src, rows_b], wire.at[src + 1, rows_b], across)

    def gather_step(k):
        count_hop(k)
        gather_hop(k, 0)
        gather_hop(k, 1)

    def gradient(*distances):
        first = order(distances[0])

        @pl.loop(2 * first, 2 * (first + len(distances)))
        def _(q):
            hidden_local(q).wait()
            hidden_remote(q).wait_recv()
            parts[q] = lax.dot_general(
                held[q], grads_in[...], (((0,), (0,)), ((), ())), preferred_element_type=F32
            )

        for d in distances:
            o = order(d)

            def stage(r, o=o):
                send_y[o, pl.ds(r, STEP)] = parts[2 * o + 1, pl.ds(ROWS_A + r, STEP)].astype(BF16)

            loop_rows(ROWS_B, stage)

    def part_y(*distances):
        for d in distances:
            send(("ry", d), send_y.at[order(d)], recv_y.at[order(d)], across)

    def reduce_far(p):
        for s in (1, -1):
            def stage(r, s=s):
                here = parts[slot(4, p), pl.ds(r, STEP), cols[s]]
                send_z[0 if s == 1 else 1, 3, pl.ds(p * BLOCK + r, STEP), cols[s]] = here.astype(BF16)

            def stage_b(r, s=s):
                here = parts[slot(4, p), pl.ds(ROWS_A + r, STEP), cols[s]]
                here = here + recv_y[order(4), pl.ds(r, STEP), cols[s]].astype(F32)
                send_z[0 if s == 1 else 1, 3, pl.ds(ROWS_A + r, STEP), cols[s]] = here.astype(BF16)

            loop_rows(ROWS_A, stage)
            if p == 0:
                if s == 1:
                    arrived(("ry", 4))
                loop_rows(ROWS_B, stage_b)
            rows = pl.ds(0, BLOCK) if p == 0 else pl.ds(BLOCK, ROWS_A)
            w = 0 if s == 1 else 1
            send(("rz", s, 4, p), send_z.at[w, 3, rows, cols[s]], recv_z.at[w, 3, rows, cols[s]], toward[s])

    def reduce_hop(d, p):
        for s in (1, -1):
            w = 0 if s == 1 else 1
            arrived(("rz", s, d + 1, p))
            if p == 0:
                arrived(("ry", s * d))

            def put(r, base, with_y, s=s, w=w):
                here = parts[slot(s * d, p), pl.ds(base + r, STEP)]
                at = pl.ds(p * BLOCK + base + r, STEP)
                if with_y:
                    here = here + recv_y[order(s * d), pl.ds(r, STEP)].astype(F32)
                if d == 3:
                    lo = 0 if s == 1 else half
                    there = recv_z[w, d, at, cols[s]].astype(F32)
                    summed = here[:, lo:lo + half] + there
                    send_z[w, d - 1, at, cols[s]] = summed.astype(BF16)
                    send_z[w, d - 1, at, cols[-s]] = here[:, half - lo:2 * half - lo].astype(BF16)
                else:
                    there = recv_z[w, d, at].astype(F32)
                    send_z[w, d - 1, at] = (here + there).astype(BF16)

            loop_rows(ROWS_A, lambda r: put(r, 0, False))
            if p == 0:
                loop_rows(ROWS_B, lambda r: put(r, ROWS_A, True))
            rows = pl.ds(0, BLOCK) if p == 0 else pl.ds(BLOCK, ROWS_A)
            send(("rz", s, d, p), send_z.at[w, d - 1, rows], recv_z.at[w, d - 1, rows], toward[s])

    def keys(*distances):
        for d in distances:
            q = slot(d, 0)
            if d == 0:
                arrived("ayB0")
            elif d == 4:
                arrived(("ayB", 4, 1))
                arrived(("ayB", 4, -1))
            else:
                arrived(("ayB", q))
            acc[...] += jnp.dot(held[q], wire[q], preferred_element_type=F32) + jnp.dot(
                held[q + 1], wire[q + 1], preferred_element_type=F32
            )

    arrived("mask")
    gradient(4)
    part_y(4)
    reduce_far(1)
    count_hop(1)
    arrived("ay0")
    gather_hop(1, 1)
    send("ayB0", wire.at[own, rows_b], wire.at[slot(0, 1), rows_b], across)
    gradient(3, -3)
    part_y(3, -3)
    count_hop(2)
    gather_hop(2, 0)
    reduce_far(0)
    gather_hop(2, 1)
    difference_x()
    gradient(2, -2)
    part_y(2, -2)
    reduce_hop(3, 1)
    reduce_hop(3, 0)
    gather_step(3)
    difference_y()
    gradient(1, -1, 0)
    part_y(1, -1)
    acc[...] = jnp.zeros_like(acc)
    reduce_hop(2, 1)
    gather_step(4)
    reduce_hop(2, 0)
    keys(0)
    reduce_hop(1, 1)
    count_column()
    for s in (1, -1):
        arrived(("az", s, 4, 0))
        src = slot(4, 0)
        send(("ayB", 4, s), wire.at[src, rows_b, cols[s]], wire.at[src + 1, rows_b, cols[s]], across)
    part_y(0)
    keys(1, -1)
    reduce_hop(1, 0)
    keys(2, -2, 3, -3)
    for e in range(1, NX):
        arrived(("dg", e))
    delta_out[...] = delta[...]

    for s in (1, -1):
        arrived(("rz", s, 1, 1))

    def close_a(r):
        at = pl.ds(BLOCK + r, STEP)
        total = parts[slot(0, 1), pl.ds(r, STEP)] + recv_z[0, 0, at].astype(F32) + recv_z[1, 0, at].astype(F32)
        send_a[pl.ds(r, STEP)] = total.astype(BF16)

    loop_rows(ROWS_A, close_a)
    send("rya", send_a, recv_a, across)
    for s in (1, -1):
        arrived(("az", s, 4, 1))
    arrived("count_across")
    scale = ((1.0 / math.sqrt(D)) / (count_total[...] + count_across[...]))[0:1, 0:1]
    keys(4)
    send("keys", acc.at[pl.ds(tok, tok)], other, mate)
    arrived("keys")

    def close_keys(r):
        at = pl.ds(r, STEP)
        keys_out[at] = ((acc[at] + other[at]) * (1.0 / math.sqrt(D))).astype(BF16)

    loop_rows(tok, close_keys)
    for s in (1, -1):
        arrived(("rz", s, 1, 0))
    arrived(("ry", 0))

    def close_b(r):
        at = pl.ds(ROWS_A + r, STEP)
        total = parts[slot(0, 0), at] + recv_y[order(0), pl.ds(r, STEP)].astype(F32)
        grad_out[at] = (total + recv_z[0, 0, at].astype(F32) + recv_z[1, 0, at].astype(F32)) * scale

    loop_rows(ROWS_B, close_b)
    arrived("rya")

    def close_all(r):
        at = pl.ds(r, STEP)
        total = parts[slot(0, 0), at] + recv_a[at].astype(F32)
        grad_out[at] = (total + recv_z[0, 0, at].astype(F32) + recv_z[1, 0, at].astype(F32)) * scale

    loop_rows(ROWS_A, close_all)
    for copy in copies.values():
        copy.wait_send()

    @pl.loop(0, 16)
    def _(q):
        hidden_remote(q).wait_send()


def exchange(hidden, tokens, key_grad, weights, anchor, fragment):
    tok, width = key_grad.shape
    half = width // 2
    vmem = pl.BlockSpec(memory_space=pltpu.VMEM)
    smem = pl.BlockSpec(memory_space=pltpu.SMEM)
    anywhere = pl.BlockSpec(memory_space=pl.ANY)
    hbm = pl.BlockSpec(memory_space=pltpu.HBM)
    count = 96
    tile = pltpu.VMEM((8, 128), F32)
    return pl.pallas_call(
        kernel,
        out_shape=(
            jax.ShapeDtypeStruct((BLOCK, width), F32),
            jax.ShapeDtypeStruct((tok, width), BF16),
            jax.ShapeDtypeStruct((BLOCK, half), F32),
        ),
        in_specs=[hbm] * 5 + [smem],
        out_specs=(vmem, vmem, vmem),
        scratch_shapes=[
            pltpu.VMEM((16, 2 * tok, BLOCK), BF16),
            pltpu.VMEM((2 * tok, width), BF16),
            pltpu.VMEM((16, BLOCK, width), F32),
            pltpu.VMEM((16, BLOCK, width), BF16),
            pltpu.VMEM((2 * tok, width), F32),
            pltpu.VMEM((tok, width), F32),
            pltpu.VMEM((2, 4, BLOCK + ROWS_A, width), BF16),
            pltpu.VMEM((2, 4, BLOCK + ROWS_A, width), BF16),
            pltpu.VMEM((8, ROWS_B, width), BF16),
            pltpu.VMEM((8, ROWS_B, width), BF16),
            pltpu.VMEM((ROWS_A, width), BF16),
            pltpu.VMEM((ROWS_A, width), BF16),
            pltpu.VMEM((tok, width), BF16),
            pltpu.VMEM((BLOCK, width), F32),
            pltpu.VMEM((BLOCK, width), F32),
            pltpu.VMEM(tokens.shape, jnp.int32),
            pltpu.VMEM((BLOCK, half), F32),
            pltpu.VMEM((NX - 1, BLOCK // NX, half), F32),
            pltpu.VMEM((BLOCK // NX, half), F32),
            pltpu.VMEM((BLOCK // NX, half), F32),
            pltpu.VMEM((BLOCK, half), F32),
            pltpu.VMEM((NZ, 8, 128), F32),
            tile,
            tile,
            tile,
            tile,
            pltpu.SemaphoreType.DMA((16,)),
            pltpu.SemaphoreType.DMA((4,)),
            pltpu.SemaphoreType.DMA((count,)),
            pltpu.SemaphoreType.DMA((count,)),
            pltpu.SemaphoreType.DMA((16,)),
            pltpu.SemaphoreType.DMA((16,)),
        ],
        compiler_params=pltpu.CompilerParams(
            collective_id=0, has_side_effects=True, vmem_limit_bytes=46 * 2**20
        ),
        cost_estimate=pl.CostEstimate(flops=13 * 10**9, bytes_accessed=16 * 2**20, transcendentals=0),
    )(hidden, tokens, key_grad, weights, anchor, fragment)


def finish_kernel(
    grad, delta, keys, first, second, weights, anchor, momentum, fragment, step_count,
    keys_out, weights_out, first_out, second_out, anchor_out, momentum_out,
    new_weights, new_first, new_second, new_anchor, new_momentum, sems,
):
    rows, width = grad.shape
    half = width // 2
    part = rows // FINISH_PARTS
    writes = [pltpu.make_async_copy(keys, keys_out, sems.at[0])]
    writes[0].start()

    def write(src, dst, at):
        writes.append(pltpu.make_async_copy(src.at[at], dst.at[at], sems.at[len(writes)]))
        writes[-1].start()

    steps = jnp.full((1, half), step_count[0], jnp.int32).astype(F32)
    first_scale = 1.0 / (1.0 - jnp.exp(steps * math.log(BETA_ONE)))
    second_scale = 1.0 / (1.0 - jnp.exp(steps * math.log(BETA_TWO)))
    for i in range(FINISH_PARTS):
        at = pl.ds(i * part, part)
        gap = delta[at]
        for h in range(FRAGS):
            cols = pl.ds(h * half, half)
            moved = fragment[0] == h
            old_anchor, old_momentum = anchor[at, cols], momentum[at, cols]
            moved_momentum = OUTER_MOMENTUM * old_momentum + gap
            moved_anchor = old_anchor - OUTER_LR * (gap + OUTER_MOMENTUM * moved_momentum)
            new_momentum[at, cols] = jnp.where(moved, moved_momentum, old_momentum)
            new_anchor[at, cols] = jnp.where(moved, moved_anchor, old_anchor)
            gradient = grad[at, cols]
            one = BETA_ONE * first[at, cols] + (1.0 - BETA_ONE) * gradient
            two = BETA_TWO * second[at, cols] + (1.0 - BETA_TWO) * gradient * gradient
            new_first[at, cols] = one
            new_second[at, cols] = two
            ratio = one * first_scale / (jnp.sqrt(two * second_scale) + EPSILON)
            old = weights[at, cols]
            stepped = old - INNER_LR * (ratio + WEIGHT_DECAY * old)
            mixed = MIX_LOCAL * stepped + (1.0 - MIX_LOCAL) * moved_anchor
            new_weights[at, cols] = jnp.where(moved, mixed, stepped)
        write(new_momentum, momentum_out, at)
        write(new_anchor, anchor_out, at)
        write(new_first, first_out, at)
        write(new_second, second_out, at)
        write(new_weights, weights_out, at)
    for copy in writes:
        copy.wait()


FINISH_PARTS = 4


def finish(grad, delta, keys, first, second, weights, anchor, momentum, fragment, step_count):
    vmem = pl.BlockSpec(memory_space=pltpu.VMEM)
    smem = pl.BlockSpec(memory_space=pltpu.SMEM)
    anywhere = pl.BlockSpec(memory_space=pl.ANY)
    block = jax.ShapeDtypeStruct(grad.shape, F32)
    return pl.pallas_call(
        finish_kernel,
        out_shape=(jax.ShapeDtypeStruct(keys.shape, keys.dtype),) + (block,) * 5,
        in_specs=[vmem, vmem, anywhere] + [vmem] * 5 + [smem, smem],
        out_specs=(anywhere,) * 6,
        scratch_shapes=[pltpu.VMEM(grad.shape, F32)] * 5 + [pltpu.SemaphoreType.DMA((1 + 5 * FINISH_PARTS,))],
        compiler_params=pltpu.CompilerParams(vmem_limit_bytes=16 * 2**20),
    )(grad, delta, keys, first, second, weights, anchor, momentum, fragment, step_count)


def on_device(
    hidden,
    token_ids,
    key_grad,
    weights,
    first_moment,
    second_moment,
    anchor,
    momentum,
    fragment,
    step_count,
):
    operands = [
        pltpu.with_memory_space_constraint(operand, pltpu.HBM)
        for operand in (hidden[0], token_ids, key_grad[0], weights[0], anchor)
    ]
    grad, keys, delta = exchange(*operands, fragment)
    keys, new_weights, new_first, new_second, new_anchor, new_momentum = finish(
        grad, delta, keys, first_moment[0], second_moment[0], weights[0], anchor, momentum, fragment, step_count
    )
    return keys[None], new_weights[None], new_first[None], new_second[None], new_anchor, new_momentum


def solution(mesh):
    return jax.shard_map(
        on_device,
        mesh=mesh,
        in_specs=(
            P("rep", "fsdp", None),
            P("rep", "fsdp"),
            P("rep", "fsdp", None),
            P("rep", "fsdp", None),
            P("rep", "fsdp", None),
            P("rep", "fsdp", None),
            P("fsdp", None),
            P("fsdp", None),
            P(),
            P(),
        ),
        out_specs=(
            P("rep", "fsdp", None),
            P("rep", "fsdp", None),
            P("rep", "fsdp", None),
            P("rep", "fsdp", None),
            P("fsdp", None),
            P("fsdp", None),
        ),
        check_vma=False,
    )
```
